256 devices in a mesh: tm: 16 (over x, y), pts: 16 (over z, core).
Axes of the slice: x: 4, y: 4, z: 8, core: 2. Of those that a mesh axis runs over, the one named last changes fastest.
Arguments:
- feats: bfloat16 [16, 4096, 256], P('tm', 'pts'), may hold values from -24 to 24
- query_frame: int32 [16384], P('pts'), may hold values from 0 to 15
- query_pos: int32 [16384], P('pts'), may hold values from 0 to 4095
- time_mix: float32 [16, 16], replicated, may hold values from -1.5 to 1.5
- w_up: bfloat16 [512, 2048], replicated, may hold values from -0.25 to 0.25
- w_down: bfloat16 [2048, 512], replicated, may hold values from -0.125 to 0.125
- w_query: bfloat16 [512, 256], replicated, may hold values from -0.25 to 0.25
Outputs:
- track_x: float32 [16, 16384], P('tm', 'pts')
- track_y: float32 [16, 16384], P('tm', 'pts')
The draws below stay inside these ranges and needn't reach their ends.
All inputs are finite; a program needn't handle non-finite values.
Results may differ from the reference program's by a relative error of at most 0.04.
Values may be sent and summed in bfloat16 or wider, within the bound.
No kernel may reach another device: no remote copies, remote signals or barrier semaphores. Data moves between devices by JAX's collectives and lax.ppermute only.
A program may use at most 64 MiB of HBM per device.

```python
import math
import jax
import jax.numpy as jnp
import numpy as np
from jax import lax

C = 256
GRID = 64
FFW = 2048
HW = 4096
HID = 512
F = 16
P_SIZE = 16384


def draw_feats(key, part):
    key = jax.random.fold_in(key, 11)
    base = jnp.clip(jax.random.normal(key, (F, HW, C), jnp.float32), -6.0, 6.0)
    return base.astype(jnp.bfloat16)


def place_ends(entries, rng, low, largest):
    longest = entries.shape.index(max(entries.shape))
    spots = []
    for shift in (0, 1):
        where = [jax.random.randint(jax.random.fold_in(rng, axis), (), 0, length) for axis, length in enumerate(entries.shape)]
        where[longest] = (where[longest] + shift) % entries.shape[longest]
        spots.append(tuple(where))
    return entries.at[spots[0]].set(low).at[spots[1]].set(largest)


def cumulative_ranks(number_of, slope):
    loads = [(1 << 20) // math.isqrt(rank ** slope) + 1 for rank in range(1, number_of + 1)]
    deviation = 1 + sum(loads) // (1 << 30)
    return np.cumsum(np.array([max(1, weight // deviation) for weight in loads]))


def skewed_ids(own_key, shape, number_of, slope):
    listing = cumulative_ranks(number_of, slope)
    lot = jax.random.randint(jax.random.fold_in(own_key, 1), shape, 0, int(listing[number_of - 1]))
    standing = jnp.searchsorted(jnp.asarray(listing, jnp.int32), lot, side="right")
    return jax.random.permutation(jax.random.fold_in(own_key, 2), number_of)[standing].astype(jnp.int32)


def scatter_about(rng, extent, deviation, limit, held_as=jnp.bfloat16):
    return jnp.clip(deviation * jax.random.normal(rng, extent, jnp.float32), -limit, limit).astype(held_as)


def setup_inputs(seed: int = 0) -> dict:
    arg_keys = jax.random.split(jax.random.key(seed), 8)
    feats = draw_feats(jax.random.fold_in(arg_keys[7], 71), 0)
    query_frame = place_ends(skewed_ids(arg_keys[1], (P_SIZE,), F, 2), jax.random.fold_in(arg_keys[1], 3), 0, F - 1).astype(jnp.int32)
    query_pos = place_ends(jax.random.randint(arg_keys[2], (P_SIZE,), 0, HW), jax.random.fold_in(arg_keys[2], 1), 0, HW - 1).astype(jnp.int32)
    time_mix = scatter_about(arg_keys[3], (F, F), F ** -0.5, 1.5, jnp.float32)
    w_up = scatter_about(arg_keys[4], (HID, FFW), HID ** -0.5, 0.25)
    w_down = scatter_about(arg_keys[5], (FFW, HID), FFW ** -0.5, 0.125)
    w_query = scatter_about(arg_keys[6], (HID, C), HID ** -0.5, 0.25)
    return {"feats": feats, "query_frame": query_frame, "query_pos": query_pos, "time_mix": time_mix, "w_up": w_up, "w_down": w_down, "w_query": w_query}


def rms_rows(values):
    return values * lax.rsqrt(lax.optimization_barrier(jnp.mean(values * values, axis=-1, keepdims=True)) + 1e-06)

def mixer(tokens, time_mix, w_up, w_down, w_query):
    frames, count, width = tokens.shape
    floats = tokens.astype(jnp.float32)
    normed = rms_rows(floats).astype(jnp.bfloat16)
    blended = jnp.einsum('fg,gkd->fkd', time_mix, normed.astype(jnp.float32), precision=lax.Precision.HIGHEST)
    section = (floats + blended).astype(jnp.bfloat16)
    flat = section.reshape(frames * count, width)
    inner = rms_rows(flat.astype(jnp.float32)).astype(jnp.bfloat16)
    upper = jax.nn.gelu(jnp.dot(inner, w_up, preferred_element_type=jnp.float32)).astype(jnp.bfloat16)
    mixed = (flat.astype(jnp.float32) + jnp.dot(upper, w_down, preferred_element_type=jnp.float32)).astype(jnp.bfloat16)
    delta = jnp.dot(mixed, w_query, preferred_element_type=jnp.float32).astype(jnp.bfloat16)
    return delta.reshape(frames, count, w_query.shape[1])

def grid_coords():
    index = jnp.arange(HW, dtype=jnp.int32)
    xs = (2 * (index % GRID) + 1).astype(jnp.float32) / GRID - 1.0
    ys = (2 * (index // GRID) + 1).astype(jnp.float32) / GRID - 1.0
    return (xs, ys)

def soft_weights(rows, frame):
    scores = jnp.dot(rows, frame.T, preferred_element_type=jnp.float32) * C ** (-0.5)
    top = lax.optimization_barrier(jnp.max(scores, axis=1, keepdims=True))
    expo = jnp.exp(scores - top)
    return (expo, lax.optimization_barrier(jnp.sum(expo, axis=1, keepdims=True)))

def reference(feats, query_frame, query_pos, time_mix, w_up, w_down, w_query):
    block = math.gcd(P_SIZE, 1024)
    xs, ys = grid_coords()

    def one_block(index):
        start = (index * block).astype(jnp.int32)
        frame_ids = lax.dynamic_slice_in_dim(query_frame, start, block)
        pos_ids = lax.dynamic_slice_in_dim(query_pos, start, block)
        query = feats[frame_ids, pos_ids]

        def match(frame):
            expo, total = soft_weights(query, frame)
            matched = (jnp.dot(expo.astype(jnp.bfloat16), frame, preferred_element_type=jnp.float32) / total).astype(jnp.bfloat16)
            return jnp.concatenate([matched, query], axis=1)
        tokens = lax.map(match, feats)
        delta = mixer(tokens, time_mix, w_up, w_down, w_query)
        refined = (query.astype(jnp.float32)[None] + delta.astype(jnp.float32)).astype(jnp.bfloat16)

        def rematch(pair):
            frame, rows = pair
            expo, total = soft_weights(rows, frame)
            return (lax.optimization_barrier(jnp.sum(expo * xs, axis=1)) / total[:, 0], lax.optimization_barrier(jnp.sum(expo * ys, axis=1)) / total[:, 0])
        return lax.map(rematch, (feats, refined))
    along_x, along_y = lax.map(one_block, jnp.arange(P_SIZE // block, dtype=jnp.int32))
    track_x = along_x.transpose(1, 0, 2).reshape(F, P_SIZE)
    track_y = along_y.transpose(1, 0, 2).reshape(F, P_SIZE)
    return (track_x, track_y)
```

```python
import jax
import jax.numpy as jnp
from jax import lax
from jax.sharding import PartitionSpec as P

GRID = 64
HW = 4096


def rms_rows(values):
    return values * lax.rsqrt(jnp.mean(values * values, axis=-1, keepdims=True) + 1e-06)


def mixer(tokens, time_mix, w_up, w_down, w_query):
    frames, count, width = tokens.shape
    floats = tokens.astype(jnp.float32)
    normed = rms_rows(floats).astype(jnp.bfloat16)
    blended = jnp.einsum(
        "fg,gkd->fkd", time_mix, normed.astype(jnp.float32), precision=lax.Precision.HIGHEST
    )
    section = (floats + blended).astype(jnp.bfloat16)
    flat = section.reshape(frames * count, width)
    inner = rms_rows(flat.astype(jnp.float32)).astype(jnp.bfloat16)
    upper = jax.nn.gelu(jnp.dot(inner, w_up, preferred_element_type=jnp.float32)).astype(
        jnp.bfloat16
    )
    mixed = (
        flat.astype(jnp.float32) + jnp.dot(upper, w_down, preferred_element_type=jnp.float32)
    ).astype(jnp.bfloat16)
    delta = jnp.dot(mixed, w_query, preferred_element_type=jnp.float32).astype(jnp.bfloat16)
    return delta.reshape(frames, count, w_query.shape[1])


def row_scores(rows, piece, scale):
    return jnp.einsum("pc,jc->pj", rows, piece, preferred_element_type=jnp.float32) * scale


def soft_parts(scores):
    top = jnp.max(scores, axis=1, keepdims=True)
    expo = jnp.exp(scores - top)
    return (expo, jnp.sum(expo, axis=1, keepdims=True))


def ring_pairs(chips, step):
    return [
        (chip * 2 + core, (chip + step) % chips * 2 + core)
        for chip in range(chips)
        for core in range(2)
    ]


def swap_pairs(chips):
    return [(chip * 2 + core, chip * 2 + 1 - core) for chip in range(chips) for core in range(2)]


def gather_frame(tile, core):
    chips = lax.axis_size("pts") // 2
    swap = swap_pairs(chips)

    def both(own):
        other = lax.ppermute(own, "pts", swap)
        even = core == 0
        return [jnp.where(even, own, other), jnp.where(even, other, own)]

    found = {0: both(tile)}
    below = above = tile
    for step in range(1, chips // 2 + 1):
        below = lax.ppermute(below, "pts", ring_pairs(chips, 1))
        if step < chips // 2:
            above = lax.ppermute(above, "pts", ring_pairs(chips, -1))
            found[step] = both(above)
        found[chips - step] = both(below)
    return jnp.concatenate([piece for at in range(chips) for piece in found[at]], axis=0)


def shards(feats, query_frame, query_pos, time_mix, w_up, w_down, w_query):
    tile = feats[0]
    points = query_frame.shape[0]
    width = tile.shape[1]
    scale = width ** (-0.5)
    frame_id = lax.axis_index("tm")
    groups = lax.axis_size("tm")
    place = lax.axis_index("pts")
    first_pos = place // 2 * 2 * tile.shape[0]
    block = min(512, points)
    frame = gather_frame(tile, place % 2)
    index = (jnp.arange(HW, dtype=jnp.int32) + first_pos) % HW
    xs = (2 * (index % GRID) + 1).astype(jnp.float32) / GRID - 1.0
    ys = (2 * (index // GRID) + 1).astype(jnp.float32) / GRID - 1.0
    picked = jnp.take(frame, (query_pos - first_pos) % HW, axis=0)
    own = jnp.where((query_frame == frame_id)[:, None], picked, jnp.zeros_like(picked))
    share = points // groups
    parts = lax.all_to_all(own.reshape(groups, share, width), "tm", 0, 0, tiled=True)
    query_here = jnp.sum(parts.astype(jnp.float32), axis=0).astype(jnp.bfloat16)
    query = lax.all_to_all(
        jnp.broadcast_to(query_here, (groups, share, width)), "tm", 0, 0, tiled=True
    ).reshape(points, width)
    pieces = []
    for first in range(0, points, block):
        expo, total = soft_parts(row_scores(query[first : first + block], frame, scale))
        product = jnp.dot(expo.astype(jnp.bfloat16), frame, preferred_element_type=jnp.float32)
        pieces.append((product / total).astype(jnp.bfloat16))
    matched = jnp.concatenate(pieces, axis=0).reshape(groups, share, width)
    matched = lax.all_to_all(matched, "tm", 0, 0, tiled=True)
    tokens = jnp.concatenate([matched, jnp.broadcast_to(query_here, matched.shape)], axis=2)
    delta = mixer(tokens, time_mix, w_up, w_down, w_query)
    returned = lax.all_to_all(delta, "tm", 0, 0, tiled=True).reshape(points, width)
    refined = (query.astype(jnp.float32) + returned.astype(jnp.float32)).astype(jnp.bfloat16)
    parts_x = []
    parts_y = []
    for first in range(0, points, block):
        expo, total = soft_parts(row_scores(refined[first : first + block], frame, scale))
        parts_x.append(jnp.sum(expo * xs, axis=1) / total[:, 0])
        parts_y.append(jnp.sum(expo * ys, axis=1) / total[:, 0])
    track_x = jnp.concatenate(parts_x, axis=0)
    track_y = jnp.concatenate(parts_y, axis=0)
    return (track_x[None], track_y[None])


def solution(mesh):
    placed = (P("tm", "pts", None), P("pts"), P("pts"), P(), P(), P(), P())
    return jax.shard_map(
        shards,
        mesh=mesh,
        in_specs=placed,
        out_specs=(P("tm", "pts"), P("tm", "pts")),
        check_vma=False,
    )
```

```python
import functools

import jax
import jax.numpy as jnp
from jax import lax
from jax.experimental import pallas as pl
from jax.experimental.pallas import tpu as pltpu
from jax.sharding import PartitionSpec as P

GRID = 64
LOG2E=1.4426950408889634
VM=pl.BlockSpec(memory_space=pltpu.VMEM)
SM=pl.BlockSpec(memory_space=pltpu.SMEM)
NT=(((1,),(1,)),((),()))
def params(mb=40): return pltpu.CompilerParams(vmem_limit_bytes=mb<<20)

def pick_kernel(n, bases_ref, want_ref, *refs):
    tiles, out = refs[:n], refs[n]
    want = want_ref[...]
    acc = None
    for t in range(n):
        rows = tiles[t].shape[0]
        rel = want - bases_ref[t]
        hot = (rel == lax.broadcasted_iota(jnp.int32, (1, rows), 1)).astype(jnp.float32).astype(jnp.bfloat16)
        part = jnp.dot(hot, tiles[t][...], preferred_element_type=jnp.float32)
        acc = part if acc is None else acc + part
    out[...] = acc.astype(jnp.bfloat16)
def pick(bases, want, tiles):
    n=len(tiles)
    return pl.pallas_call(functools.partial(pick_kernel,n),
        out_shape=jax.ShapeDtypeStruct((want.shape[0],tiles[0].shape[1]),jnp.bfloat16),
        in_specs=[SM]+[VM]*(n+1), out_specs=VM, compiler_params=params())(bases,want,*tiles)

def match_kernel(n, bp, k, q_ref, *refs):
    tiles, out, bufs = refs[:n], refs[n], refs[n+1:]
    w = tiles[0].shape[0]
    blocks = q_ref.shape[0]//bp
    def score(i, t, m):
        s = lax.dot_general(q_ref[i*bp:(i+1)*bp], tiles[t][...], NT, preferred_element_type=jnp.float32)
        bufs[i%2][:, t*w:(t+1)*w] = s
        for h in range(0,w,128):
            m = s[:,h:h+128] if m is None else jnp.maximum(m, s[:,h:h+128])
        return m
    m=None
    for t in range(n): m=score(0,t,m)
    for i in range(blocks):
        top = jnp.max(m,axis=1,keepdims=True)*k
        m=None; acc=None; tot=None
        for t in range(n):
            if i+1<blocks: m=score(i+1,t,m)
            e = jnp.exp2(bufs[i%2][:, t*w:(t+1)*w]*k - top)
            for h in range(0,w,128):
                tot = e[:,h:h+128] if tot is None else tot+e[:,h:h+128]
            p = jnp.dot(e.astype(jnp.bfloat16), tiles[t][...], preferred_element_type=jnp.float32)
            acc = p if acc is None else acc+p
        total = jnp.sum(tot,axis=1,keepdims=True)
        out[i*bp:(i+1)*bp] = (acc/total).astype(jnp.bfloat16)
def match(q, tiles, bp=256):
    n=len(tiles); k=LOG2E*q.shape[1]**-0.5
    return pl.pallas_call(functools.partial(match_kernel,n,bp,k),
        out_shape=jax.ShapeDtypeStruct(q.shape,jnp.bfloat16),
        in_specs=[VM]*(n+1), out_specs=VM,
        scratch_shapes=[pltpu.VMEM((bp,n*tiles[0].shape[0]),jnp.float32)]*2, compiler_params=params())(q,*tiles)

def rematch_kernel(n, bp, k, grid, bases_ref, q_ref, *refs):
    tiles, ox, oy, bufs = refs[:n], refs[n], refs[n+1], refs[n+2:]
    w = tiles[0].shape[0]
    blocks = q_ref.shape[0]//bp
    lines = w//grid
    def score(i, t, m):
        s = lax.dot_general(tiles[t][...], q_ref[i*bp:(i+1)*bp], NT, preferred_element_type=jnp.float32)
        bufs[i%2][t*w:(t+1)*w] = s
        p = jnp.max(s.reshape(w//8,8,bp),axis=0)
        return p if m is None else jnp.maximum(m,p)
    xs = (2*lax.broadcasted_iota(jnp.int32,(grid,1),0)+1).astype(jnp.float32)/grid-1.0
    m=None
    for t in range(n): m=score(0,t,m)
    for i in range(blocks):
        top = jnp.max(m,axis=0,keepdims=True)*k
        m=None; cols=None; ysum=None
        for t in range(n):
            if i+1<blocks: m=score(i+1,t,m)
            line0 = bases_ref[t]//grid
            for r in range(lines):
                e = jnp.exp2(bufs[i%2][t*w+r*grid:t*w+(r+1)*grid]*k - top)
                cols = e if cols is None else cols+e
                y = (2*(line0+r)+1).astype(jnp.float32)/grid-1.0
                part = jnp.sum(e.reshape(grid//8,8,bp),axis=0)*y
                ysum = part if ysum is None else ysum+part
        total = jnp.sum(cols,axis=0,keepdims=True)
        ox[:,i*bp:(i+1)*bp] = jnp.sum(cols*xs,axis=0,keepdims=True)/total
        oy[:,i*bp:(i+1)*bp] = jnp.sum(ysum,axis=0,keepdims=True)/total
def rematch(bases, q, tiles, grid=64, bp=256):
    n=len(tiles); k=LOG2E*q.shape[1]**-0.5
    return pl.pallas_call(functools.partial(rematch_kernel,n,bp,k,grid),
        out_shape=[jax.ShapeDtypeStruct((1,q.shape[0]),jnp.float32)]*2,
        in_specs=[SM]+[VM]*(n+1), out_specs=[VM]*2,
        scratch_shapes=[pltpu.VMEM((n*tiles[0].shape[0],bp),jnp.float32)]*2, compiler_params=params())(bases,q,*tiles)

def prep_kernel(tm_ref, wd_ref, wq_ref, big_ref, fold_ref):
    f = tm_ref.shape[0]
    side = big_ref.shape[1]
    rep = side//f
    spread = (lax.broadcasted_iota(jnp.int32,(side,f),0)//rep == lax.broadcasted_iota(jnp.int32,(side,f),1)).astype(jnp.float32).astype(jnp.bfloat16)
    same = lax.broadcasted_iota(jnp.int32,(side,side),0)%rep == lax.broadcasted_iota(jnp.int32,(side,side),1)%rep
    rest = tm_ref[...]
    for part in range(big_ref.shape[0]):
        now = rest.astype(jnp.bfloat16)
        rest = rest - now.astype(jnp.float32)
        rows = jnp.dot(spread, now, preferred_element_type=jnp.float32).astype(jnp.bfloat16)
        full = lax.dot_general(rows, spread, NT, preferred_element_type=jnp.float32)
        big_ref[part] = jnp.where(same, full, 0.0).astype(jnp.bfloat16)
    fold_ref[...] = jnp.dot(wd_ref[...], wq_ref[...], preferred_element_type=jnp.float32).astype(jnp.bfloat16)
def prep(time_mix, w_down, w_query, parts=2):
    return pl.pallas_call(prep_kernel,
        out_shape=[jax.ShapeDtypeStruct((parts,256,256),jnp.bfloat16), jax.ShapeDtypeStruct((w_down.shape[0],w_query.shape[1]),jnp.bfloat16)],
        in_specs=[VM]*3, out_specs=[VM]*2, compiler_params=params())(time_mix,w_down,w_query)

def mixer_kernel(hid, m_ref, q_ref, big_ref, up_ref, fold_ref, wq_ref, out_ref):
    frames, points, width = m_ref.shape
    side = big_ref.shape[1]
    rep = side//frames
    for j in range(points//rep):
        here = slice(j*rep,(j+1)*rep)
        q = q_ref[here]
        both = jnp.concatenate([jnp.concatenate([m_ref[f,here] for f in range(frames)],axis=0),
                                jnp.concatenate([q]*frames,axis=0)],axis=1).astype(jnp.float32)
        normed = (both*lax.rsqrt(jnp.mean(both*both,axis=1,keepdims=True)+1e-6)).astype(jnp.bfloat16)
        sec = both
        for part in range(big_ref.shape[0]):
            sec = sec + jnp.dot(big_ref[part], normed, preferred_element_type=jnp.float32)
        sec16 = sec.astype(jnp.bfloat16)
        sec = sec16.astype(jnp.float32)
        inner = (sec*lax.rsqrt(jnp.mean(sec*sec,axis=1,keepdims=True)+1e-6)).astype(jnp.bfloat16)
        acc = jnp.dot(sec16, wq_ref[...], preferred_element_type=jnp.float32)
        for h in range(0, up_ref.shape[1], hid):
            u = jnp.dot(inner, up_ref[:,h:h+hid], preferred_element_type=jnp.float32)
            u = jax.nn.gelu(u).astype(jnp.bfloat16)
            acc = acc + jnp.dot(u, fold_ref[h:h+hid], preferred_element_type=jnp.float32)
        delta = acc.astype(jnp.bfloat16).astype(jnp.float32)
        q32 = q.astype(jnp.float32)
        for f in range(frames):
            out_ref[f,here] = (q32 + delta[f*rep:(f+1)*rep]).astype(jnp.bfloat16)
def mixer(m, q, big, w_up, fold, w_query, hid=256):
    return pl.pallas_call(functools.partial(mixer_kernel,hid),
        out_shape=jax.ShapeDtypeStruct(m.shape,jnp.bfloat16),
        in_specs=[VM]*6, out_specs=VM, compiler_params=params())(m,q,big,w_up,fold,w_query)


def ring_pairs(chips, step):
    return [
        (chip * 2 + core, (chip + step) % chips * 2 + core)
        for chip in range(chips)
        for core in range(2)
    ]


def swap_pairs(chips):
    return [(chip * 2 + core, chip * 2 + 1 - core) for chip in range(chips) for core in range(2)]


def gather_tiles(tile):
    chips = lax.axis_size("pts") // 2
    swap = swap_pairs(chips)
    found = {0: [tile, lax.ppermute(tile, "pts", swap)]}
    below = above = tile
    for step in range(1, chips // 2 + 1):
        below = lax.ppermute(below, "pts", ring_pairs(chips, 1))
        if step < chips // 2:
            above = lax.ppermute(above, "pts", ring_pairs(chips, -1))
            found[step] = [above, lax.ppermute(above, "pts", swap)]
        found[chips - step] = [below, lax.ppermute(below, "pts", swap)]
    tiles = [piece for at in range(chips) for piece in found[at]]
    place = lax.axis_index("pts")
    chip = (place // 2 + jnp.arange(chips, dtype=jnp.int32)) % chips
    core = jnp.array([0, 1], jnp.int32)
    bases = (chip[:, None] * 2 + (core + place) % 2) * tile.shape[0]
    return (tiles, bases.reshape(-1))


def shards(feats, query_frame, query_pos, time_mix, w_up, w_down, w_query):
    tile = feats[0]
    points = query_frame.shape[0]
    width = tile.shape[1]
    frame_id = lax.axis_index("tm")
    groups = lax.axis_size("tm")
    share = points // groups
    tiles, bases = gather_tiles(tile)
    want = jnp.where(query_frame == frame_id, query_pos, -1).reshape(points, 1)
    own = pick(bases, want, tiles)
    parts = lax.all_to_all(own.reshape(groups, share, width), "tm", 0, 0, tiled=True)
    query_here = jnp.sum(parts.astype(jnp.float32), axis=0).astype(jnp.bfloat16)
    query = lax.all_to_all(
        jnp.broadcast_to(query_here, (groups, share, width)), "tm", 0, 0, tiled=True
    ).reshape(points, width)
    mixes, folded = prep(time_mix, w_down, w_query)
    matched = match(query, tiles).reshape(groups, share, width)
    matched = lax.all_to_all(matched, "tm", 0, 0, tiled=True)
    refined = mixer(matched, query_here, mixes, w_up, folded, w_query)
    refined = lax.all_to_all(refined, "tm", 0, 0, tiled=True).reshape(points, width)
    return rematch(bases, refined, tiles, GRID)


def solution(mesh):
    placed = (P("tm", "pts", None), P("pts"), P("pts"), P(), P(), P(), P())
    return jax.shard_map(
        shards,
        mesh=mesh,
        in_specs=placed,
        out_specs=(P("tm", "pts"), P("tm", "pts")),
        check_vma=False,
    )
```

```python
import functools

import jax
import jax.numpy as jnp
from jax import lax
from jax.experimental import pallas as pl
from jax.experimental.pallas import tpu as pltpu
from jax.sharding import PartitionSpec as P

GRID = 64
LOG2E = 1.4426950408889634
IN_VMEM = pl.BlockSpec(memory_space=pltpu.VMEM)
IN_SMEM = pl.BlockSpec(memory_space=pltpu.SMEM)
ANYWHERE = pl.BlockSpec(memory_space=pl.ANY)
NT = (((1,), (1,)), ((), ()))


def params(megabytes):
    return pltpu.CompilerParams(vmem_limit_bytes=megabytes << 20)


def cost(macs, nbytes):
    return pl.CostEstimate(flops=2 * macs, bytes_accessed=nbytes, transcendentals=0)


def pick_kernel(count, bases_ref, want_ref, *refs):
    tiles, before, out = refs[:count], refs[count:-1], refs[-1]
    want = want_ref[...]
    total = None
    for t, tile in enumerate(tiles):
        rows = tile.shape[0]
        lane = lax.broadcasted_iota(jnp.int32, (1, rows), 1)
        hot = (want - bases_ref[t] == lane).astype(jnp.float32).astype(jnp.bfloat16)
        part = jnp.dot(hot, tile[...], preferred_element_type=jnp.float32)
        total = part if total is None else total + part
    for other in before:
        total = total + other[...].astype(jnp.float32)
    out[...] = total.astype(jnp.bfloat16)


def pick(bases, want, tiles, before=()):
    points, width = want.shape[0], tiles[0].shape[1]
    count = len(tiles)
    return pl.pallas_call(
        functools.partial(pick_kernel, count),
        out_shape=jax.ShapeDtypeStruct((points, width), jnp.bfloat16),
        in_specs=[IN_SMEM] + [IN_VMEM] * (1 + count + len(before)),
        out_specs=IN_VMEM,
        compiler_params=params(12),
        cost_estimate=cost(points * count * tiles[0].size, 2 * count * tiles[0].size),
        name="pick",
    )(bases, want, *tiles, *before)


def tile_copies(tiles, frame_ref, sems):
    rows = tiles[0].shape[0]
    copies = [
        pltpu.make_async_copy(tile, frame_ref.at[pl.ds(t * rows, rows)], sems.at[t])
        for t, tile in enumerate(tiles)
    ]
    for copy in copies:
        copy.start()
    return copies


def match_kernel(count, block, factor, q_ref, *refs):
    tiles, out = refs[:count], refs[count]
    frame_ref, even, odd, sems = refs[count + 1 :]
    bufs = (even, odd)
    rows = tiles[0].shape[0]
    blocks = q_ref.shape[0] // block
    copies = tile_copies(tiles, frame_ref, sems)

    def score(i, t, top):
        s = lax.dot_general(
            q_ref[i * block : (i + 1) * block],
            frame_ref[t * rows : (t + 1) * rows],
            NT,
            preferred_element_type=jnp.float32,
        )
        bufs[i % 2][:, t * rows : (t + 1) * rows] = s
        for h in range(0, rows, 128):
            top = s[:, h : h + 128] if top is None else jnp.maximum(top, s[:, h : h + 128])
        return top

    top = None
    for t in range(count):
        copies[t].wait()
        top = score(0, t, top)
    for i in range(blocks):
        high = jnp.max(top, axis=1, keepdims=True) * factor
        top = acc = sums = None
        for t in range(count):
            if i + 1 < blocks:
                top = score(i + 1, t, top)
            expo = jnp.exp2(bufs[i % 2][:, t * rows : (t + 1) * rows] * factor - high)
            for h in range(0, rows, 128):
                sums = expo[:, h : h + 128] if sums is None else sums + expo[:, h : h + 128]
            part = jnp.dot(
                expo.astype(jnp.bfloat16),
                frame_ref[t * rows : (t + 1) * rows],
                preferred_element_type=jnp.float32,
            )
            acc = part if acc is None else acc + part
        total = jnp.sum(sums, axis=1, keepdims=True)
        out[i * block : (i + 1) * block] = (acc / total).astype(jnp.bfloat16)


def match(query, tiles, block=256):
    points, width = query.shape
    count = len(tiles)
    places = count * tiles[0].shape[0]
    return pl.pallas_call(
        functools.partial(match_kernel, count, block, LOG2E * width**-0.5),
        out_shape=jax.ShapeDtypeStruct(query.shape, jnp.bfloat16),
        in_specs=[IN_VMEM] + [ANYWHERE] * count,
        out_specs=IN_VMEM,
        scratch_shapes=[
            pltpu.VMEM((places, width), jnp.bfloat16),
            pltpu.VMEM((block, places), jnp.float32),
            pltpu.VMEM((block, places), jnp.float32),
            pltpu.SemaphoreType.DMA((count,)),
        ],
        compiler_params=params(20),
        cost_estimate=cost(2 * points * places * width, 2 * places * width),
        name="match",
    )(query, *tiles)


def rematch_kernel(count, block, factor, bases_ref, q_ref, *refs):
    tiles, out_x, out_y, frame_ref, sems = refs[:count], *refs[count:]
    rows = tiles[0].shape[0]
    blocks = q_ref.shape[0] // block
    copies = tile_copies(tiles, frame_ref, sems)
    sub = lax.broadcasted_iota(jnp.int32, (8, 1), 0)
    columns = [(2 * (sub + at) + 1).astype(jnp.float32) / GRID - 1.0 for at in range(0, GRID, 8)]
    for i in range(blocks):
        top = None
        total = sum_x = sum_y = jnp.zeros((8, block), jnp.float32)
        for t in range(count):
            if i == 0:
                copies[t].wait()
            s = lax.dot_general(
                frame_ref[t * rows : (t + 1) * rows],
                q_ref[i * block : (i + 1) * block],
                NT,
                preferred_element_type=jnp.float32,
            ).reshape(rows // 8, 8, block)
            high = jnp.max(s, axis=0)
            if top is not None:
                high = jnp.maximum(high, top)
                shrink = jnp.exp2((top - high) * factor)
                total, sum_x, sum_y = total * shrink, sum_x * shrink, sum_y * shrink
            top = high
            high = high * factor
            first = bases_ref[t] // GRID
            for line in range(rows // GRID):
                y = (2 * (first + line) + 1).astype(jnp.float32) / GRID - 1.0
                here = None
                for c, x in enumerate(columns):
                    expo = jnp.exp2(s[line * len(columns) + c] * factor - high)
                    sum_x = sum_x + expo * x
                    here = expo if here is None else here + expo
                total = total + here
                sum_y = sum_y + here * y
        weight = jnp.exp2((top - jnp.max(top, axis=0, keepdims=True)) * factor)
        total = jnp.sum(total * weight, axis=0, keepdims=True)
        here = slice(i * block, (i + 1) * block)
        out_x[:, here] = jnp.sum(sum_x * weight, axis=0, keepdims=True) / total
        out_y[:, here] = jnp.sum(sum_y * weight, axis=0, keepdims=True) / total


def rematch(bases, refined, tiles, block=256):
    points, width = refined.shape
    count = len(tiles)
    places = count * tiles[0].shape[0]
    return pl.pallas_call(
        functools.partial(rematch_kernel, count, block, LOG2E * width**-0.5),
        out_shape=[jax.ShapeDtypeStruct((1, points), jnp.float32)] * 2,
        in_specs=[IN_SMEM, IN_VMEM] + [ANYWHERE] * count,
        out_specs=[IN_VMEM] * 2,
        scratch_shapes=[
            pltpu.VMEM((places, width), jnp.bfloat16),
            pltpu.SemaphoreType.DMA((count,)),
        ],
        compiler_params=params(12),
        cost_estimate=cost(points * places * width, 2 * places * width),
        name="rematch",
    )(bases, refined, *tiles)


def prep_kernel(mix_ref, down_ref, to_query_ref, mixes_ref, folded_ref):
    frames = mix_ref.shape[0]
    side = mixes_ref.shape[1]
    repeat = side // frames

    def iota(shape, axis):
        return lax.broadcasted_iota(jnp.int32, shape, axis)

    spread = iota((side, frames), 0) // repeat == iota((side, frames), 1)
    spread = spread.astype(jnp.float32).astype(jnp.bfloat16)
    same = iota((side, side), 0) % repeat == iota((side, side), 1) % repeat
    rest = mix_ref[...]
    for part in range(mixes_ref.shape[0]):
        now = rest.astype(jnp.bfloat16)
        rest = rest - now.astype(jnp.float32)
        rows = jnp.dot(spread, now, preferred_element_type=jnp.float32).astype(jnp.bfloat16)
        full = lax.dot_general(rows, spread, NT, preferred_element_type=jnp.float32)
        mixes_ref[part] = jnp.where(same, full, 0.0).astype(jnp.bfloat16)
    folded_ref[...] = jnp.dot(
        down_ref[...], to_query_ref[...], preferred_element_type=jnp.float32
    ).astype(jnp.bfloat16)


def prep(time_mix, w_down, w_query, side=256, parts=2):
    hidden, width = w_down.shape
    return pl.pallas_call(
        prep_kernel,
        out_shape=[
            jax.ShapeDtypeStruct((parts, side, side), jnp.bfloat16),
            jax.ShapeDtypeStruct((hidden, w_query.shape[1]), jnp.bfloat16),
        ],
        in_specs=[IN_VMEM] * 3,
        out_specs=[IN_VMEM] * 2,
        compiler_params=params(10),
        cost_estimate=cost(w_down.size * w_query.shape[1], 2 * w_down.size),
        name="prep",
    )(time_mix, w_down, w_query)


def mixer_kernel(step, m_ref, q_ref, mixes_any, up_any, folded_any, tq_any, out_ref, *scratch):
    mixes_ref, up_ref, folded_ref, tq_ref, sems = scratch
    frames, points, width = m_ref.shape
    side = mixes_ref.shape[1]
    repeat = side // frames
    hidden = up_ref.shape[1]
    weights = [
        pltpu.make_async_copy(source, target, sems.at[n])
        for n, (source, target) in enumerate(
            [(mixes_any, mixes_ref), (tq_any, tq_ref), (up_any, up_ref), (folded_any, folded_ref)]
        )
    ]
    for copy in weights:
        copy.start()
    for j in range(points // repeat):
        here = slice(j * repeat, (j + 1) * repeat)
        query = q_ref[here]
        matched = jnp.concatenate([m_ref[f, here] for f in range(frames)], axis=0)
        tokens = jnp.concatenate(
            [matched, jnp.concatenate([query] * frames, axis=0)], axis=1
        ).astype(jnp.float32)
        power = jnp.mean(tokens * tokens, axis=1, keepdims=True)
        normed = (tokens * lax.rsqrt(power + 1e-06)).astype(jnp.bfloat16)
        if j == 0:
            weights[0].wait()
        section = tokens
        for part in range(mixes_ref.shape[0]):
            section = section + jnp.dot(
                mixes_ref[part], normed, preferred_element_type=jnp.float32
            )
        kept = section.astype(jnp.bfloat16)
        section = kept.astype(jnp.float32)
        power = jnp.mean(section * section, axis=1, keepdims=True)
        inner = (section * lax.rsqrt(power + 1e-06)).astype(jnp.bfloat16)
        if j == 0:
            weights[1].wait()
        acc = jnp.dot(kept, tq_ref[...], preferred_element_type=jnp.float32)
        if j == 0:
            weights[2].wait()
            weights[3].wait()
        for h in range(0, hidden, step):
            upper = jnp.dot(inner, up_ref[:, h : h + step], preferred_element_type=jnp.float32)
            upper = jax.nn.gelu(upper).astype(jnp.bfloat16)
            acc = acc + jnp.dot(
                upper, folded_ref[h : h + step], preferred_element_type=jnp.float32
            )
        delta = acc.astype(jnp.bfloat16).astype(jnp.float32)
        query = query.astype(jnp.float32)
        for f in range(frames):
            out_ref[f, here] = (query + delta[f * repeat : (f + 1) * repeat]).astype(jnp.bfloat16)


def mixer(matched, query, mixes, w_up, folded, w_query, step=256):
    return pl.pallas_call(
        functools.partial(mixer_kernel, step),
        out_shape=jax.ShapeDtypeStruct(matched.shape, jnp.bfloat16),
        in_specs=[IN_VMEM] * 2 + [ANYWHERE] * 4,
        out_specs=IN_VMEM,
        scratch_shapes=[
            pltpu.VMEM(array.shape, array.dtype) for array in (mixes, w_up, folded, w_query)
        ]
        + [pltpu.SemaphoreType.DMA((4,))],
        compiler_params=params(16),
        cost_estimate=cost(matched.shape[0] * matched.shape[1] * (w_up.size + folded.size), 2 * w_up.size),
        name="mixer",
    )(matched, query, mixes, w_up, folded, w_query)


def ring_pairs(chips, step):
    return [
        (chip * 2 + core, (chip + step) % chips * 2 + core)
        for chip in range(chips)
        for core in range(2)
    ]


def swap_pairs(chips):
    return [(chip * 2 + core, chip * 2 + 1 - core) for chip in range(chips) for core in range(2)]


def shards(feats, query_frame, query_pos, time_mix, w_up, w_down, w_query):
    tile = feats[0]
    points = query_frame.shape[0]
    rows, width = tile.shape
    frame_id = lax.axis_index("tm")
    groups = lax.axis_size("tm")
    share = points // groups
    chips = lax.axis_size("pts") // 2
    place = lax.axis_index("pts")
    want = jnp.where(query_frame == frame_id, query_pos, -1).reshape(points, 1)
    swap = swap_pairs(chips)
    tiles = []
    bases = []

    def add(piece, away):
        tiles.extend([piece, lax.ppermute(piece, "pts", swap)])
        chip = (place // 2 + away + chips) % chips
        bases.extend([(chip * 2 + place % 2) * rows, (chip * 2 + 1 - place % 2) * rows])

    add(tile, 0)
    below = above = tile
    own = ()
    done = 0
    for step in range(1, chips // 2 + 1):
        below = lax.ppermute(below, "pts", ring_pairs(chips, 1))
        if step < chips // 2:
            above = lax.ppermute(above, "pts", ring_pairs(chips, -1))
            add(above, step)
        add(below, -step)
        if step != 1:
            own = (pick(jnp.stack(bases[done:]), want, tiles[done:], own),)
            done = len(tiles)
    bases = jnp.stack(bases)
    parts = lax.all_to_all(own[0].reshape(groups, share, width), "tm", 0, 0, tiled=True)
    query_here = jnp.sum(parts.astype(jnp.float32), axis=0).astype(jnp.bfloat16)
    query = lax.all_to_all(
        jnp.broadcast_to(query_here, (groups, share, width)), "tm", 0, 0, tiled=True
    ).reshape(points, width)
    mixes, folded = prep(time_mix, w_down, w_query)
    matched = match(query, tiles).reshape(groups, share, width)
    matched = lax.all_to_all(matched, "tm", 0, 0, tiled=True)
    refined = mixer(matched, query_here, mixes, w_up, folded, w_query)
    refined = lax.all_to_all(refined, "tm", 0, 0, tiled=True).reshape(points, width)
    return rematch(bases, refined, tiles)


def solution(mesh):
    placed = (P("tm", "pts", None), P("pts"), P("pts"), P(), P(), P(), P())
    return jax.shard_map(
        shards,
        mesh=mesh,
        in_specs=placed,
        out_specs=(P("tm", "pts"), P("tm", "pts")),
        check_vma=False,
    )
```

```python
import functools

import jax
import jax.numpy as jnp
from jax import lax
from jax.experimental import pallas as pl
from jax.experimental.pallas import tpu as pltpu
from jax.sharding import PartitionSpec as P

GRID = 64
LOG2E = 1.4426950408889634
IN_VMEM = pl.BlockSpec(memory_space=pltpu.VMEM)
NT = (((1,), (1,)), ((), ()))


def params(megabytes):
    return pltpu.CompilerParams(vmem_limit_bytes=megabytes << 20)


def cost(macs, nbytes):
    return pl.CostEstimate(flops=2 * macs, bytes_accessed=nbytes, transcendentals=0)


def tile_bases(aways, rows):
    chips = lax.axis_size("pts") // 2
    place = lax.axis_index("pts")
    core = lax.rem(place, 2)
    bases = []
    for away in aways:
        chip = lax.rem(place // 2 + (away + chips) % chips, chips)
        bases += [(chip * 2 + core) * rows, (chip * 2 + 1 - core) * rows]
    return bases


def pick_kernel(aways, frame_ref, pos_ref, *refs):
    count = 2 * len(aways)
    tiles, before, out = refs[:count], refs[count:-1], refs[-1]
    points = pos_ref.shape[1]
    want = jnp.where(frame_ref[...] == lax.axis_index("tm"), pos_ref[...], -1)
    spread = []
    for first in range(0, points, 128):
        row = jnp.broadcast_to(want[:, first : first + 128], (128, 128))
        spread.append(jnp.transpose(row))
    want = jnp.concatenate(spread, axis=0)
    lane = lax.broadcasted_iota(jnp.int32, (1, 128), 1)
    total = None
    for tile, base in zip(tiles, tile_bases(aways, tiles[0].shape[0])):
        hot = jnp.concatenate(
            [
                (want == lane + (base + first)).astype(jnp.float32).astype(jnp.bfloat16)
                for first in range(0, tile.shape[0], 128)
            ],
            axis=1,
        )
        part = jnp.dot(hot, tile[...], preferred_element_type=jnp.float32)
        total = part if total is None else total + part
    for other in before:
        total = total + other[...].astype(jnp.float32)
    out[...] = total.astype(jnp.bfloat16)


def pick(query_frame, query_pos, aways, tiles, before=()):
    points, width = query_pos.shape[1], tiles[0].shape[1]
    count = len(tiles)
    return pl.pallas_call(
        functools.partial(pick_kernel, aways),
        out_shape=jax.ShapeDtypeStruct((points, width), jnp.bfloat16),
        in_specs=[IN_VMEM] * (2 + count + len(before)),
        out_specs=IN_VMEM,
        compiler_params=params(12),
        cost_estimate=cost(points * count * tiles[0].size, 2 * count * tiles[0].size),
        name="pick",
    )(query_frame, query_pos, *tiles, *before)


def join_kernel(parts_ref, query_ref, copies_ref):
    query = jnp.sum(parts_ref[...].astype(jnp.float32), axis=0).astype(jnp.bfloat16)
    query_ref[...] = query
    for n in range(copies_ref.shape[0]):
        copies_ref[n] = query


def join(parts):
    return pl.pallas_call(
        join_kernel,
        out_shape=[
            jax.ShapeDtypeStruct(parts.shape[1:], parts.dtype),
            jax.ShapeDtypeStruct(parts.shape, parts.dtype),
        ],
        in_specs=[IN_VMEM],
        out_specs=[IN_VMEM] * 2,
        compiler_params=params(6),
        cost_estimate=cost(parts.size, 4 * parts.size),
        name="join",
    )(parts)


def match_kernel(count, block, factor, q_ref, *refs):
    tiles, out, bufs = refs[:count], refs[count], refs[count + 1 :]
    rows = tiles[0].shape[0]
    blocks = q_ref.shape[0] // block

    def score(i, t, top):
        s = lax.dot_general(
            q_ref[i * block : (i + 1) * block],
            tiles[t][...],
            NT,
            preferred_element_type=jnp.float32,
        )
        bufs[i % 2][:, t * rows : (t + 1) * rows] = s
        for h in range(0, rows, 128):
            top = s[:, h : h + 128] if top is None else jnp.maximum(top, s[:, h : h + 128])
        return top

    top = None
    for t in range(count):
        top = score(0, t, top)
    for i in range(blocks):
        high = jnp.max(top, axis=1, keepdims=True) * factor
        top = acc = sums = None
        for t in range(count):
            if i + 1 < blocks:
                top = score(i + 1, t, top)
            expo = jnp.exp2(bufs[i % 2][:, t * rows : (t + 1) * rows] * factor - high)
            for h in range(0, rows, 128):
                sums = expo[:, h : h + 128] if sums is None else sums + expo[:, h : h + 128]
            part = jnp.dot(
                expo.astype(jnp.bfloat16), tiles[t][...], preferred_element_type=jnp.float32
            )
            acc = part if acc is None else acc + part
        total = jnp.sum(sums, axis=1, keepdims=True)
        out[i * block : (i + 1) * block] = (acc / total).astype(jnp.bfloat16)


def match(query, tiles, block=256):
    points, width = query.shape
    count = len(tiles)
    places = count * tiles[0].shape[0]
    return pl.pallas_call(
        functools.partial(match_kernel, count, block, LOG2E * width**-0.5),
        out_shape=jax.ShapeDtypeStruct(query.shape, jnp.bfloat16),
        in_specs=[IN_VMEM] * (1 + count),
        out_specs=IN_VMEM,
        scratch_shapes=[pltpu.VMEM((block, places), jnp.float32)] * 2,
        compiler_params=params(18),
        cost_estimate=cost(2 * points * places * width, 2 * places * width),
        name="match",
    )(query, *tiles)


def rematch_kernel(aways, block, factor, q_ref, *refs):
    tiles, out_x, out_y = refs[:-2], refs[-2], refs[-1]
    count = len(tiles)
    rows = tiles[0].shape[0]
    bases = tile_bases(aways, rows)
    sub = lax.broadcasted_iota(jnp.int32, (8, 1), 0)
    columns = [(2 * (sub + at) + 1).astype(jnp.float32) / GRID - 1.0 for at in range(0, GRID, 8)]
    work = [(i, t) for i in range(q_ref.shape[0] // block) for t in range(count)]

    def score(i, t):
        return lax.dot_general(
            tiles[t][...],
            q_ref[i * block : (i + 1) * block],
            NT,
            preferred_element_type=jnp.float32,
        ).reshape(rows // 8, 8, block)

    ahead = score(*work[0])
    for n, (i, t) in enumerate(work):
        s = ahead
        if n + 1 < len(work):
            ahead = score(*work[n + 1])
        if t == 0:
            top = None
            sums = [None] * len(columns)
            sum_y = jnp.zeros((8, block), jnp.float32)
        high = jnp.max(s, axis=0)
        if top is not None:
            high = jnp.maximum(high, top)
            shrink = jnp.exp2((top - high) * factor)
            sum_y = sum_y * shrink
            sums = [value * shrink for value in sums]
        top = high
        high = high * factor
        first = bases[t] // GRID
        for line in range(rows // GRID):
            y = (2 * (first + line) + 1).astype(jnp.float32) / GRID - 1.0
            here = None
            for c in range(len(columns)):
                expo = jnp.exp2(s[line * len(columns) + c] * factor - high)
                sums[c] = expo if sums[c] is None else sums[c] + expo
                here = expo if here is None else here + expo
            sum_y = sum_y + here * y
        if t == count - 1:
            total = sums[0]
            sum_x = sums[0] * columns[0]
            for value, x in zip(sums[1:], columns[1:]):
                total = total + value
                sum_x = sum_x + value * x
            weight = jnp.exp2((top - jnp.max(top, axis=0, keepdims=True)) * factor)
            total = jnp.sum(total * weight, axis=0, keepdims=True)
            here = slice(i * block, (i + 1) * block)
            out_x[:, here] = jnp.sum(sum_x * weight, axis=0, keepdims=True) / total
            out_y[:, here] = jnp.sum(sum_y * weight, axis=0, keepdims=True) / total


def rematch(refined, aways, tiles, block=256):
    points, width = refined.shape
    count = len(tiles)
    places = count * tiles[0].shape[0]
    return pl.pallas_call(
        functools.partial(rematch_kernel, aways, block, LOG2E * width**-0.5),
        out_shape=[jax.ShapeDtypeStruct((1, points), jnp.float32)] * 2,
        in_specs=[IN_VMEM] * (1 + count),
        out_specs=[IN_VMEM] * 2,
        compiler_params=params(12),
        cost_estimate=cost(points * places * width, 2 * places * width),
        name="rematch",
    )(refined, *tiles)


def prep_kernel(mix_ref, down_ref, to_query_ref, mixes_ref, folded_ref):
    frames = mix_ref.shape[0]
    side = mixes_ref.shape[1]
    repeat = side // frames

    def iota(shape, axis):
        return lax.broadcasted_iota(jnp.int32, shape, axis)

    spread = iota((side, frames), 0) // repeat == iota((side, frames), 1)
    spread = spread.astype(jnp.float32).astype(jnp.bfloat16)
    same = iota((side, side), 0) % repeat == iota((side, side), 1) % repeat
    rest = mix_ref[...]
    for part in range(mixes_ref.shape[0]):
        now = rest.astype(jnp.bfloat16)
        rest = rest - now.astype(jnp.float32)
        rows = jnp.dot(spread, now, preferred_element_type=jnp.float32).astype(jnp.bfloat16)
        full = lax.dot_general(rows, spread, NT, preferred_element_type=jnp.float32)
        mixes_ref[part] = jnp.where(same, full, 0.0).astype(jnp.bfloat16)
    folded_ref[...] = jnp.dot(
        down_ref[...], to_query_ref[...], preferred_element_type=jnp.float32
    ).astype(jnp.bfloat16)


def prep(time_mix, w_down, w_query, side=256, parts=2):
    hidden, width = w_down.shape
    return pl.pallas_call(
        prep_kernel,
        out_shape=[
            jax.ShapeDtypeStruct((parts, side, side), jnp.bfloat16),
            jax.ShapeDtypeStruct((hidden, w_query.shape[1]), jnp.bfloat16),
        ],
        in_specs=[IN_VMEM] * 3,
        out_specs=[IN_VMEM] * 2,
        compiler_params=params(10),
        cost_estimate=cost(w_down.size * w_query.shape[1], 2 * w_down.size),
        name="prep",
    )(time_mix, w_down, w_query)


def mixer_kernel(step, m_ref, q_ref, mixes_ref, up_ref, folded_ref, tq_ref, out_ref):
    frames, points, width = m_ref.shape
    side = mixes_ref.shape[1]
    repeat = side // frames
    hidden = up_ref.shape[1]
    for j in range(points // repeat):
        here = slice(j * repeat, (j + 1) * repeat)
        query = q_ref[here]
        matched = jnp.concatenate([m_ref[f, here] for f in range(frames)], axis=0)
        tokens = jnp.concatenate(
            [matched, jnp.concatenate([query] * frames, axis=0)], axis=1
        ).astype(jnp.float32)
        power = jnp.mean(tokens * tokens, axis=1, keepdims=True)
        normed = (tokens * lax.rsqrt(power + 1e-06)).astype(jnp.bfloat16)
        section = tokens
        for part in range(mixes_ref.shape[0]):
            section = section + jnp.dot(
                mixes_ref[part], normed, preferred_element_type=jnp.float32
            )
        kept = section.astype(jnp.bfloat16)
        section = kept.astype(jnp.float32)
        power = jnp.mean(section * section, axis=1, keepdims=True)
        inner = (section * lax.rsqrt(power + 1e-06)).astype(jnp.bfloat16)
        acc = jnp.dot(kept, tq_ref[...], preferred_element_type=jnp.float32)
        for h in range(0, hidden, step):
            upper = jnp.dot(inner, up_ref[:, h : h + step], preferred_element_type=jnp.float32)
            upper = jax.nn.gelu(upper).astype(jnp.bfloat16)
            acc = acc + jnp.dot(
                upper, folded_ref[h : h + step], preferred_element_type=jnp.float32
            )
        delta = acc.astype(jnp.bfloat16).astype(jnp.float32)
        query = query.astype(jnp.float32)
        for f in range(frames):
            out_ref[f, here] = (query + delta[f * repeat : (f + 1) * repeat]).astype(jnp.bfloat16)


def mixer(matched, query, mixes, w_up, folded, w_query, step=256):
    return pl.pallas_call(
        functools.partial(mixer_kernel, step),
        out_shape=jax.ShapeDtypeStruct(matched.shape, jnp.bfloat16),
        in_specs=[IN_VMEM] * 6,
        out_specs=IN_VMEM,
        compiler_params=params(16),
        cost_estimate=cost(matched.shape[0] * matched.shape[1] * (w_up.size + folded.size), 2 * w_up.size),
        name="mixer",
    )(matched, query, mixes, w_up, folded, w_query)


def ring_pairs(chips, step):
    return [
        (chip * 2 + core, (chip + step) % chips * 2 + core)
        for chip in range(chips)
        for core in range(2)
    ]


def swap_pairs(chips):
    return [(chip * 2 + core, chip * 2 + 1 - core) for chip in range(chips) for core in range(2)]


def shards(feats, query_frame, query_pos, time_mix, w_up, w_down, w_query):
    tile = feats[0]
    points = query_frame.shape[0]
    width = tile.shape[1]
    groups = lax.axis_size("tm")
    share = points // groups
    chips = lax.axis_size("pts") // 2
    query_frame = query_frame.reshape(1, points)
    query_pos = query_pos.reshape(1, points)
    swap = swap_pairs(chips)
    tiles = []
    aways = []

    def add(piece, away):
        tiles.extend([piece, lax.ppermute(piece, "pts", swap)])
        aways.append(away)

    add(tile, 0)
    below = above = tile
    own = ()
    done = 0
    for step in range(1, chips // 2 + 1):
        below = lax.ppermute(below, "pts", ring_pairs(chips, 1))
        if step < chips // 2:
            above = lax.ppermute(above, "pts", ring_pairs(chips, -1))
            add(above, step)
        add(below, -step)
        if step != 1:
            own = (pick(query_frame, query_pos, aways[done:], tiles[2 * done :], own),)
            done = len(aways)
    parts = lax.all_to_all(own[0].reshape(groups, share, width), "tm", 0, 0, tiled=True)
    query_here, copies = join(parts)
    query = lax.all_to_all(copies, "tm", 0, 0, tiled=True).reshape(points, width)
    mixes, folded = prep(time_mix, w_down, w_query)
    matched = match(query, tiles).reshape(groups, share, width)
    matched = lax.all_to_all(matched, "tm", 0, 0, tiled=True)
    refined = mixer(matched, query_here, mixes, w_up, folded, w_query)
    refined = lax.all_to_all(refined, "tm", 0, 0, tiled=True).reshape(points, width)
    return rematch(refined, aways, tiles)


def solution(mesh):
    placed = (P("tm", "pts", None), P("pts"), P("pts"), P(), P(), P(), P())
    return jax.shard_map(
        shards,
        mesh=mesh,
        in_specs=placed,
        out_specs=(P("tm", "pts"), P("tm", "pts")),
        check_vma=False,
    )
```

```python
import functools

import jax
import jax.numpy as jnp
from jax import lax
from jax.experimental import pallas as pl
from jax.experimental.pallas import tpu as pltpu
from jax.sharding import PartitionSpec as P

GRID = 64
LOG2E = 1.4426950408889634
IN_VMEM = pl.BlockSpec(memory_space=pltpu.VMEM)
IN_HBM = pl.BlockSpec(memory_space=pltpu.HBM)
NT = (((1,), (1,)), ((), ()))


def params(megabytes):
    return pltpu.CompilerParams(vmem_limit_bytes=megabytes << 20)


def cost(macs, nbytes):
    return pl.CostEstimate(flops=2 * macs, bytes_accessed=nbytes, transcendentals=0)


def tile_bases(aways, rows):
    chips = lax.axis_size("pts") // 2
    place = lax.axis_index("pts")
    core = lax.rem(place, 2)
    bases = []
    for away in aways:
        chip = lax.rem(place // 2 + (away + chips) % chips, chips)
        bases += [(chip * 2 + core) * rows, (chip * 2 + 1 - core) * rows]
    return bases


def begin_kernel(tile_hbm, frame_hbm, pos_hbm, tile_out, want_ref, frame_ref, pos_ref, sems):
    pairs = [(frame_hbm, frame_ref), (pos_hbm, pos_ref), (tile_hbm, tile_out)]
    copies = [
        pltpu.make_async_copy(source, target, sems.at[n]) for n, (source, target) in enumerate(pairs)
    ]
    for copy in copies:
        copy.start()
    copies[0].wait()
    copies[1].wait()
    want = jnp.where(frame_ref[...] == lax.axis_index("tm"), pos_ref[...], -1)
    for first in range(0, want.shape[1], 128):
        row = jnp.broadcast_to(want[:, first : first + 128], (128, 128))
        want_ref[first : first + 128] = jnp.transpose(row)
    copies[2].wait()


def begin(tile, query_frame, query_pos):
    points = query_pos.shape[1]
    return pl.pallas_call(
        begin_kernel,
        out_shape=[
            jax.ShapeDtypeStruct(tile.shape, tile.dtype),
            jax.ShapeDtypeStruct((points, 128), jnp.int32),
        ],
        in_specs=[IN_HBM] * 3,
        out_specs=[IN_VMEM] * 2,
        scratch_shapes=[pltpu.VMEM((1, points), jnp.int32)] * 2 + [pltpu.SemaphoreType.DMA((3,))],
        compiler_params=params(60),
        cost_estimate=cost(points * 128, 4 * points * 128),
        name="begin",
    )(tile, query_frame, query_pos)


def pick_kernel(aways, given, sent, want_ref, *refs):
    count = 2 * len(aways)
    tiles, refs = refs[:count], refs[count:]
    before, refs = refs[:given], refs[given:]
    sources, out, targets = refs[:sent], refs[-1 - sent], refs[len(refs) - sent :]
    want = want_ref[...]
    lane = lax.broadcasted_iota(jnp.int32, (1, 128), 1)
    total = None
    for tile, base in zip(tiles, tile_bases(aways, tiles[0].shape[0])):
        hot = jnp.concatenate(
            [
                (want == lane + (base + first)).astype(jnp.float32).astype(jnp.bfloat16)
                for first in range(0, tile.shape[0], 128)
            ],
            axis=1,
        )
        part = jnp.dot(hot, tile[...], preferred_element_type=jnp.float32)
        total = part if total is None else total + part
    for other in before:
        total = total + other[...].astype(jnp.float32)
    out[...] = total.astype(jnp.bfloat16)
    for source, target in zip(sources, targets):
        target[...] = source[...]


def pick(want, aways, tiles, before=(), sent=(), after=()):
    points, width = want.shape[0], tiles[0].shape[1]
    count = len(tiles)

    def kernel(*refs):
        ahead = 1 + count + len(before) + len(sent)
        pick_kernel(aways, len(before), len(sent), *refs[:ahead], *refs[ahead + len(after) :])

    return pl.pallas_call(
        kernel,
        out_shape=[jax.ShapeDtypeStruct((points, width), jnp.bfloat16)]
        + [jax.ShapeDtypeStruct(piece.shape, piece.dtype) for piece in sent],
        in_specs=[IN_VMEM] * (1 + count + len(before) + len(sent))
        + [pl.BlockSpec(memory_space=pl.ANY)] * len(after),
        out_specs=[IN_VMEM] * (1 + len(sent)),
        compiler_params=params(12),
        cost_estimate=cost(points * count * tiles[0].size, 2 * count * tiles[0].size),
        name="pick",
    )(want, *tiles, *before, *sent, *after)


def join_kernel(parts_ref, query_ref, copies_ref):
    query = jnp.sum(parts_ref[...].astype(jnp.float32), axis=0).astype(jnp.bfloat16)
    query_ref[...] = query
    for n in range(copies_ref.shape[0]):
        copies_ref[n] = query


def join(parts):
    return pl.pallas_call(
        join_kernel,
        out_shape=[
            jax.ShapeDtypeStruct(parts.shape[1:], parts.dtype),
            jax.ShapeDtypeStruct(parts.shape, parts.dtype),
        ],
        in_specs=[IN_VMEM],
        out_specs=[IN_VMEM] * 2,
        compiler_params=params(6),
        cost_estimate=cost(parts.size, 4 * parts.size),
        name="join",
    )(parts)


def match_kernel(count, block, factor, q_ref, *refs):
    tiles, out, bufs = refs[:count], refs[count], refs[count + 1 :]
    rows = tiles[0].shape[0]
    blocks = q_ref.shape[0] // block

    def score(i, t, top):
        s = lax.dot_general(
            q_ref[i * block : (i + 1) * block],
            tiles[t][...],
            NT,
            preferred_element_type=jnp.float32,
        )
        bufs[i % 2][:, t * rows : (t + 1) * rows] = s
        for h in range(0, rows, 128):
            top = s[:, h : h + 128] if top is None else jnp.maximum(top, s[:, h : h + 128])
        return top

    top = None
    for t in range(count):
        top = score(0, t, top)
    for i in range(blocks):
        high = jnp.max(top, axis=1, keepdims=True) * factor
        top = acc = sums = None
        for t in range(count):
            if i + 1 < blocks:
                top = score(i + 1, t, top)
            expo = jnp.exp2(bufs[i % 2][:, t * rows : (t + 1) * rows] * factor - high)
            for h in range(0, rows, 128):
                sums = expo[:, h : h + 128] if sums is None else sums + expo[:, h : h + 128]
            part = jnp.dot(
                expo.astype(jnp.bfloat16), tiles[t][...], preferred_element_type=jnp.float32
            )
            acc = part if acc is None else acc + part
        total = jnp.sum(sums, axis=1, keepdims=True)
        out[i * block : (i + 1) * block] = (acc / total).astype(jnp.bfloat16)


def match(query, tiles, block=256):
    points, width = query.shape
    count = len(tiles)
    places = count * tiles[0].shape[0]
    return pl.pallas_call(
        functools.partial(match_kernel, count, block, LOG2E * width**-0.5),
        out_shape=jax.ShapeDtypeStruct(query.shape, jnp.bfloat16),
        in_specs=[IN_VMEM] * (1 + count),
        out_specs=IN_VMEM,
        scratch_shapes=[pltpu.VMEM((block, places), jnp.float32)] * 2,
        compiler_params=params(18),
        cost_estimate=cost(2 * points * places * width, 2 * places * width),
        name="match",
    )(query, *tiles)


def rematch_kernel(aways, block, factor, q_ref, *refs):
    tiles, out_x, out_y = refs[:-2], refs[-2], refs[-1]
    count = len(tiles)
    rows = tiles[0].shape[0]
    bases = tile_bases(aways, rows)
    sub = lax.broadcasted_iota(jnp.int32, (8, 1), 0)
    columns = [(2 * (sub + at) + 1).astype(jnp.float32) / GRID - 1.0 for at in range(0, GRID, 8)]
    work = [(i, t) for i in range(q_ref.shape[0] // block) for t in range(count)]

    def score(i, t):
        return lax.dot_general(
            tiles[t][...],
            q_ref[i * block : (i + 1) * block],
            NT,
            preferred_element_type=jnp.float32,
        ).reshape(rows // 8, 8, block)

    ahead = score(*work[0])
    for n, (i, t) in enumerate(work):
        s = ahead
        if n + 1 < len(work):
            ahead = score(*work[n + 1])
        if t == 0:
            top = None
            sums = [None] * len(columns)
            sum_y = jnp.zeros((8, block), jnp.float32)
        high = jnp.max(s, axis=0)
        if top is not None:
            high = jnp.maximum(high, top)
            shrink = jnp.exp2((top - high) * factor)
            sum_y = sum_y * shrink
            sums = [value * shrink for value in sums]
        top = high
        high = high * factor
        first = bases[t] // GRID
        for line in range(rows // GRID):
            y = (2 * (first + line) + 1).astype(jnp.float32) / GRID - 1.0
            here = None
            for c in range(len(columns)):
                expo = jnp.exp2(s[line * len(columns) + c] * factor - high)
                sums[c] = expo if sums[c] is None else sums[c] + expo
                here = expo if here is None else here + expo
            sum_y = sum_y + here * y
        if t == count - 1:
            total = sums[0]
            sum_x = sums[0] * columns[0]
            for value, x in zip(sums[1:], columns[1:]):
                total = total + value
                sum_x = sum_x + value * x
            weight = jnp.exp2((top - jnp.max(top, axis=0, keepdims=True)) * factor)
            total = jnp.sum(total * weight, axis=0, keepdims=True)
            here = slice(i * block, (i + 1) * block)
            out_x[:, here] = jnp.sum(sum_x * weight, axis=0, keepdims=True) / total
            out_y[:, here] = jnp.sum(sum_y * weight, axis=0, keepdims=True) / total


def rematch(refined, aways, tiles, block=256):
    points, width = refined.shape
    count = len(tiles)
    places = count * tiles[0].shape[0]
    return pl.pallas_call(
        functools.partial(rematch_kernel, aways, block, LOG2E * width**-0.5),
        out_shape=[jax.ShapeDtypeStruct((1, points), jnp.float32)] * 2,
        in_specs=[IN_VMEM] * (1 + count),
        out_specs=[IN_VMEM] * 2,
        compiler_params=params(12),
        cost_estimate=cost(points * places * width, 2 * places * width),
        name="rematch",
    )(refined, *tiles)


def prep_kernel(mix_hbm, down_hbm, tq_hbm, mixes_ref, folded_ref, token_ref, mix_ref, down_ref, tq_ref, sems):
    frames = mix_ref.shape[0]
    side = mixes_ref.shape[1]
    repeat = side // frames
    rows = down_ref.shape[0] // 8
    pieces = [pl.ds(at * rows, rows) for at in range(8)]
    copies = [
        pltpu.make_async_copy(mix_hbm, mix_ref, sems.at[0]),
        pltpu.make_async_copy(tq_hbm, tq_ref, sems.at[1]),
    ] + [
        pltpu.make_async_copy(down_hbm.at[piece], down_ref.at[piece], sems.at[2 + n])
        for n, piece in enumerate(pieces)
    ]
    for copy in copies:
        copy.start()

    def iota(shape, axis):
        return lax.broadcasted_iota(jnp.int32, shape, axis)

    spread = iota((side, frames), 0) // repeat == iota((side, frames), 1)
    spread = spread.astype(jnp.float32).astype(jnp.bfloat16)
    same = iota((side, side), 0) % repeat == iota((side, side), 1) % repeat
    copies[0].wait()
    rest = mix_ref[...]
    for part in range(mixes_ref.shape[0]):
        now = rest.astype(jnp.bfloat16)
        rest = rest - now.astype(jnp.float32)
        rows_of = jnp.dot(spread, now, preferred_element_type=jnp.float32).astype(jnp.bfloat16)
        full = lax.dot_general(rows_of, spread, NT, preferred_element_type=jnp.float32)
        mixes_ref[part] = jnp.where(same, full, 0.0).astype(jnp.bfloat16)
    token_ref[...] = jnp.zeros_like(token_ref)
    copies[1].wait()
    for n in range(8):
        copies[2 + n].wait()
        here = slice(n * rows, (n + 1) * rows)
        folded_ref[here] = jnp.dot(
            down_ref[here], tq_ref[...], preferred_element_type=jnp.float32
        ).astype(jnp.bfloat16)


def prep(time_mix, w_down, w_query, side=256, parts=2):
    hidden, width = w_down.shape
    return pl.pallas_call(
        prep_kernel,
        out_shape=[
            jax.ShapeDtypeStruct((parts, side, side), jnp.bfloat16),
            jax.ShapeDtypeStruct((hidden, w_query.shape[1]), jnp.bfloat16),
            jax.ShapeDtypeStruct((8, 128), jnp.float32),
        ],
        in_specs=[IN_HBM] * 3,
        out_specs=[IN_VMEM] * 3,
        scratch_shapes=[
            pltpu.VMEM(time_mix.shape, time_mix.dtype),
            pltpu.VMEM(w_down.shape, w_down.dtype),
            pltpu.VMEM(w_query.shape, w_query.dtype),
            pltpu.SemaphoreType.DMA((10,)),
        ],
        compiler_params=params(56),
        cost_estimate=cost(w_down.size * w_query.shape[1], 2 * w_down.size),
        name="prep",
    )(time_mix, w_down, w_query)


def mixer_kernel(step, m_ref, q_ref, mixes_ref, up_ref, folded_ref, tq_ref, out_ref):
    frames, points, width = m_ref.shape
    side = mixes_ref.shape[1]
    repeat = side // frames
    hidden = up_ref.shape[1]
    for j in range(points // repeat):
        here = slice(j * repeat, (j + 1) * repeat)
        query = q_ref[here]
        matched = jnp.concatenate([m_ref[f, here] for f in range(frames)], axis=0)
        tokens = jnp.concatenate(
            [matched, jnp.concatenate([query] * frames, axis=0)], axis=1
        ).astype(jnp.float32)
        power = jnp.mean(tokens * tokens, axis=1, keepdims=True)
        normed = (tokens * lax.rsqrt(power + 1e-06)).astype(jnp.bfloat16)
        section = tokens
        for part in range(mixes_ref.shape[0]):
            section = section + jnp.dot(
                mixes_ref[part], normed, preferred_element_type=jnp.float32
            )
        kept = section.astype(jnp.bfloat16)
        section = kept.astype(jnp.float32)
        power = jnp.mean(section * section, axis=1, keepdims=True)
        inner = (section * lax.rsqrt(power + 1e-06)).astype(jnp.bfloat16)
        acc = jnp.dot(kept, tq_ref[...], preferred_element_type=jnp.float32)
        for h in range(0, hidden, step):
            upper = jnp.dot(inner, up_ref[:, h : h + step], preferred_element_type=jnp.float32)
            upper = jax.nn.gelu(upper).astype(jnp.bfloat16)
            acc = acc + jnp.dot(
                upper, folded_ref[h : h + step], preferred_element_type=jnp.float32
            )
        delta = acc.astype(jnp.bfloat16).astype(jnp.float32)
        query = query.astype(jnp.float32)
        for f in range(frames):
            out_ref[f, here] = (query + delta[f * repeat : (f + 1) * repeat]).astype(jnp.bfloat16)


def mixer(matched, query, mixes, w_up, folded, w_query, step=256):
    return pl.pallas_call(
        functools.partial(mixer_kernel, step),
        out_shape=jax.ShapeDtypeStruct(matched.shape, jnp.bfloat16),
        in_specs=[IN_VMEM] * 6,
        out_specs=IN_VMEM,
        compiler_params=params(16),
        cost_estimate=cost(matched.shape[0] * matched.shape[1] * (w_up.size + folded.size), 2 * w_up.size),
        name="mixer",
    )(matched, query, mixes, w_up, folded, w_query)


def ring_pairs(chips, step):
    return [
        (chip * 2 + core, (chip + step) % chips * 2 + core)
        for chip in range(chips)
        for core in range(2)
    ]


def swap_pairs(chips):
    return [(chip * 2 + core, chip * 2 + 1 - core) for chip in range(chips) for core in range(2)]


def shards(feats, query_frame, query_pos, time_mix, w_up, w_down, w_query):
    points = query_frame.shape[0]
    groups = lax.axis_size("tm")
    share = points // groups
    chips = lax.axis_size("pts") // 2
    width = feats.shape[2]
    tile, want = begin(feats[0], query_frame.reshape(1, points), query_pos.reshape(1, points))
    mixes, folded, token = prep(time_mix, w_down, w_query)
    swap = swap_pairs(chips)
    up, down = ring_pairs(chips, 1), ring_pairs(chips, -1)
    half = chips // 2
    tiles = [tile, lax.ppermute(tile, "pts", swap)]
    aways = [0]
    own = []
    done = 0
    below, above = lax.ppermute(tile, "pts", up), lax.ppermute(tile, "pts", down)
    for step in range(1, half + 1):
        sent = [above, below] if step < half else [below]
        if step < half:
            below = lax.ppermute(below, "pts", up)
            above = lax.ppermute(above, "pts", down) if step + 1 < half else None
        if step > 1 and step < half:
            after = (token,) if step == 2 else ()
            picked, *sent = pick(want, aways[done:], tiles[2 * done :], own, sent, after)
            own = [picked]
            done = len(aways)
        elif step == half:
            own = pick(want, aways[done:], tiles[2 * done :], own)
            done = len(aways)
        for piece in sent:
            tiles += [piece, lax.ppermute(piece, "pts", swap)]
        aways += [step, -step] if step < half else [-step]
    own = pick(want, aways[done:], tiles[2 * done :], own)
    parts = lax.all_to_all(own[0].reshape(groups, share, width), "tm", 0, 0, tiled=True)
    query_here, copies = join(parts)
    query = lax.all_to_all(copies, "tm", 0, 0, tiled=True).reshape(points, width)
    matched = match(query, tiles).reshape(groups, share, width)
    matched = lax.all_to_all(matched, "tm", 0, 0, tiled=True)
    refined = mixer(matched, query_here, mixes, w_up, folded, w_query)
    refined = lax.all_to_all(refined, "tm", 0, 0, tiled=True).reshape(points, width)
    return rematch(refined, aways, tiles)


def solution(mesh):
    placed = (P("tm", "pts", None), P("pts"), P("pts"), P(), P(), P(), P())
    return jax.shard_map(
        shards,
        mesh=mesh,
        in_specs=placed,
        out_specs=(P("tm", "pts"), P("tm", "pts")),
        check_vma=False,
    )
```

```python
import functools

import jax
import jax.numpy as jnp
from jax import lax
from jax.experimental import pallas as pl
from jax.experimental.pallas import tpu as pltpu
from jax.sharding import PartitionSpec as P

GRID = 64
LOG2E = 1.4426950408889634
IN_VMEM = pl.BlockSpec(memory_space=pltpu.VMEM)
IN_SMEM = pl.BlockSpec(memory_space=pltpu.SMEM)
IN_HBM = pl.BlockSpec(memory_space=pltpu.HBM)
NT = (((1,), (1,)), ((), ()))


def params(megabytes):
    return pltpu.CompilerParams(vmem_limit_bytes=megabytes << 20)


def cost(macs, nbytes):
    return pl.CostEstimate(flops=2 * macs, bytes_accessed=nbytes, transcendentals=0)


def tile_bases(aways, rows):
    chips = lax.axis_size("pts") // 2
    place = lax.axis_index("pts")
    core = lax.rem(place, 2)
    bases = []
    for away in aways:
        chip = lax.rem(place // 2 + (away + chips) % chips, chips)
        bases += [(chip * 2 + core) * rows, (chip * 2 + 1 - core) * rows]
    return bases


def begin_kernel(tile_hbm, frame_hbm, pos_hbm, tile_out, want_ref, frame_ref, pos_ref, sems):
    pairs = [(frame_hbm, frame_ref), (pos_hbm, pos_ref), (tile_hbm, tile_out)]
    copies = [
        pltpu.make_async_copy(source, target, sems.at[n]) for n, (source, target) in enumerate(pairs)
    ]
    for copy in copies:
        copy.start()
    copies[0].wait()
    copies[1].wait()
    want = jnp.where(frame_ref[...] == lax.axis_index("tm"), pos_ref[...], -1)
    for first in range(0, want.shape[1], 128):
        row = jnp.broadcast_to(want[:, first : first + 128], (128, 128))
        want_ref[first : first + 128] = jnp.transpose(row)
    copies[2].wait()


def begin(tile, query_frame, query_pos):
    points = query_pos.shape[1]
    return pl.pallas_call(
        begin_kernel,
        out_shape=[
            jax.ShapeDtypeStruct(tile.shape, tile.dtype),
            jax.ShapeDtypeStruct((points, 128), jnp.int32),
        ],
        in_specs=[IN_HBM] * 3,
        out_specs=[IN_VMEM] * 2,
        scratch_shapes=[pltpu.VMEM((1, points), jnp.int32)] * 2 + [pltpu.SemaphoreType.DMA((3,))],
        compiler_params=params(60),
        cost_estimate=cost(points * 128, 4 * points * 128),
        name="begin",
    )(tile, query_frame, query_pos)


def pick_kernel(aways, given, sent, want_ref, *refs):
    count = 2 * len(aways)
    tiles, refs = refs[:count], refs[count:]
    before, refs = refs[:given], refs[given:]
    sources, out, targets = refs[:sent], refs[-1 - sent], refs[len(refs) - sent :]
    want = want_ref[...]
    lane = lax.broadcasted_iota(jnp.int32, (1, 128), 1)
    total = None
    for tile, base in zip(tiles, tile_bases(aways, tiles[0].shape[0])):
        hot = jnp.concatenate(
            [
                (want == lane + (base + first)).astype(jnp.float32).astype(jnp.bfloat16)
                for first in range(0, tile.shape[0], 128)
            ],
            axis=1,
        )
        part = jnp.dot(hot, tile[...], preferred_element_type=jnp.float32)
        total = part if total is None else total + part
    for other in before:
        total = total + other[...].astype(jnp.float32)
    out[...] = total.astype(jnp.bfloat16)
    for source, target in zip(sources, targets):
        target[...] = source[...]


def pick(want, aways, tiles, before=(), sent=(), after=()):
    points, width = want.shape[0], tiles[0].shape[1]
    count = len(tiles)

    def kernel(*refs):
        ahead = 1 + count + len(before) + len(sent)
        pick_kernel(aways, len(before), len(sent), *refs[:ahead], *refs[ahead + len(after) :])

    return pl.pallas_call(
        kernel,
        out_shape=[jax.ShapeDtypeStruct((points, width), jnp.bfloat16)]
        + [jax.ShapeDtypeStruct(piece.shape, piece.dtype) for piece in sent],
        in_specs=[IN_VMEM] * (1 + count + len(before) + len(sent))
        + [IN_SMEM] * len(after),
        out_specs=[IN_VMEM] * (1 + len(sent)),
        compiler_params=params(12),
        cost_estimate=cost(points * count * tiles[0].size, 2 * count * tiles[0].size),
        name="pick",
    )(want, *tiles, *before, *sent, *after)


def join_kernel(parts_ref, query_ref, copies_ref):
    query = jnp.sum(parts_ref[...].astype(jnp.float32), axis=0).astype(jnp.bfloat16)
    query_ref[...] = query
    for n in range(copies_ref.shape[0]):
        copies_ref[n] = query


def join(parts):
    return pl.pallas_call(
        join_kernel,
        out_shape=[
            jax.ShapeDtypeStruct(parts.shape[1:], parts.dtype),
            jax.ShapeDtypeStruct(parts.shape, parts.dtype),
        ],
        in_specs=[IN_VMEM],
        out_specs=[IN_VMEM] * 2,
        compiler_params=params(6),
        cost_estimate=cost(parts.size, 4 * parts.size),
        name="join",
    )(parts)


def match_kernel(count, block, factor, q_ref, *refs):
    tiles, out, bufs = refs[:count], refs[count], refs[count + 1 :]
    rows = tiles[0].shape[0]
    blocks = q_ref.shape[0] // block

    def score(i, t, top):
        s = lax.dot_general(
            q_ref[i * block : (i + 1) * block],
            tiles[t][...],
            NT,
            preferred_element_type=jnp.float32,
        )
        bufs[i % 2][:, t * rows : (t + 1) * rows] = s
        for h in range(0, rows, 128):
            top = s[:, h : h + 128] if top is None else jnp.maximum(top, s[:, h : h + 128])
        return top

    top = None
    for t in range(count):
        top = score(0, t, top)
    for i in range(blocks):
        high = jnp.max(top, axis=1, keepdims=True) * factor
        top = acc = sums = None
        for t in range(count):
            if i + 1 < blocks:
                top = score(i + 1, t, top)
            expo = jnp.exp2(bufs[i % 2][:, t * rows : (t + 1) * rows] * factor - high)
            for h in range(0, rows, 128):
                sums = expo[:, h : h + 128] if sums is None else sums + expo[:, h : h + 128]
            part = jnp.dot(
                expo.astype(jnp.bfloat16), tiles[t][...], preferred_element_type=jnp.float32
            )
            acc = part if acc is None else acc + part
        total = jnp.sum(sums, axis=1, keepdims=True)
        out[i * block : (i + 1) * block] = (acc / total).astype(jnp.bfloat16)


def match(query, tiles, block=256):
    points, width = query.shape
    count = len(tiles)
    places = count * tiles[0].shape[0]
    return pl.pallas_call(
        functools.partial(match_kernel, count, block, LOG2E * width**-0.5),
        out_shape=jax.ShapeDtypeStruct(query.shape, jnp.bfloat16),
        in_specs=[IN_VMEM] * (1 + count),
        out_specs=IN_VMEM,
        scratch_shapes=[pltpu.VMEM((block, places), jnp.float32)] * 2,
        compiler_params=params(18),
        cost_estimate=cost(2 * points * places * width, 2 * places * width),
        name="match",
    )(query, *tiles)


def rematch_kernel(aways, block, factor, q_ref, *refs):
    tiles, out_x, out_y = refs[:-2], refs[-2], refs[-1]
    count = len(tiles)
    rows = tiles[0].shape[0]
    bases = tile_bases(aways, rows)
    sub = lax.broadcasted_iota(jnp.int32, (8, 1), 0)
    columns = [(2 * (sub + at) + 1).astype(jnp.float32) / GRID - 1.0 for at in range(0, GRID, 8)]
    work = [(i, t) for i in range(q_ref.shape[0] // block) for t in range(count)]

    def score(i, t):
        return lax.dot_general(
            tiles[t][...],
            q_ref[i * block : (i + 1) * block],
            NT,
            preferred_element_type=jnp.float32,
        ).reshape(rows // 8, 8, block)

    ahead = score(*work[0])
    for n, (i, t) in enumerate(work):
        s = ahead
        if n + 1 < len(work):
            ahead = score(*work[n + 1])
        if t == 0:
            top = None
            sums = [None] * len(columns)
            sum_y = jnp.zeros((8, block), jnp.float32)
        high = jnp.max(s, axis=0)
        if top is not None:
            high = jnp.maximum(high, top)
            shrink = jnp.exp2((top - high) * factor)
            sum_y = sum_y * shrink
            sums = [value * shrink for value in sums]
        top = high
        high = high * factor
        first = bases[t] // GRID
        for line in range(rows // GRID):
            y = (2 * (first + line) + 1).astype(jnp.float32) / GRID - 1.0
            here = None
            for c in range(len(columns)):
                expo = jnp.exp2(s[line * len(columns) + c] * factor - high)
                sums[c] = expo if sums[c] is None else sums[c] + expo
                here = expo if here is None else here + expo
            sum_y = sum_y + here * y
        if t == count - 1:
            total = sums[0]
            sum_x = sums[0] * columns[0]
            for value, x in zip(sums[1:], columns[1:]):
                total = total + value
                sum_x = sum_x + value * x
            weight = jnp.exp2((top - jnp.max(top, axis=0, keepdims=True)) * factor)
            total = jnp.sum(total * weight, axis=0, keepdims=True)
            here = slice(i * block, (i + 1) * block)
            out_x[:, here] = jnp.sum(sum_x * weight, axis=0, keepdims=True) / total
            out_y[:, here] = jnp.sum(sum_y * weight, axis=0, keepdims=True) / total


def rematch(refined, aways, tiles, block=256):
    points, width = refined.shape
    count = len(tiles)
    places = count * tiles[0].shape[0]
    return pl.pallas_call(
        functools.partial(rematch_kernel, aways, block, LOG2E * width**-0.5),
        out_shape=[jax.ShapeDtypeStruct((1, points), jnp.float32)] * 2,
        in_specs=[IN_VMEM] * (1 + count),
        out_specs=[IN_VMEM] * 2,
        compiler_params=params(12),
        cost_estimate=cost(points * places * width, 2 * places * width),
        name="rematch",
    )(refined, *tiles)


def prep_kernel(mix_hbm, down_hbm, tq_hbm, mixes_hbm, folded_hbm, token_ref, *scratch):
    mixes_ref, folded_ref, mix_ref, down_ref, tq_ref, sems_in, sems_out = scratch
    frames = mix_ref.shape[0]
    side = mixes_ref.shape[1]
    repeat = side // frames
    count = sems_in.shape[0] - 2
    rows = down_ref.shape[0] // count
    pieces = [pl.ds(at * rows, rows) for at in range(count)]
    loads = [
        pltpu.make_async_copy(mix_hbm, mix_ref, sems_in.at[0]),
        pltpu.make_async_copy(tq_hbm, tq_ref, sems_in.at[1]),
    ] + [
        pltpu.make_async_copy(down_hbm.at[piece], down_ref.at[piece], sems_in.at[2 + n])
        for n, piece in enumerate(pieces)
    ]
    saves = [
        pltpu.make_async_copy(folded_ref.at[piece], folded_hbm.at[piece], sems_out.at[n])
        for n, piece in enumerate(pieces)
    ] + [pltpu.make_async_copy(mixes_ref, mixes_hbm, sems_out.at[count])]
    for copy in loads:
        copy.start()

    def iota(shape, axis):
        return lax.broadcasted_iota(jnp.int32, shape, axis)

    spread = iota((side, frames), 0) // repeat == iota((side, frames), 1)
    spread = spread.astype(jnp.float32).astype(jnp.bfloat16)
    same = iota((side, side), 0) % repeat == iota((side, side), 1) % repeat
    loads[0].wait()
    rest = mix_ref[...]
    for part in range(mixes_ref.shape[0]):
        now = rest.astype(jnp.bfloat16)
        rest = rest - now.astype(jnp.float32)
        rows_of = jnp.dot(spread, now, preferred_element_type=jnp.float32).astype(jnp.bfloat16)
        full = lax.dot_general(rows_of, spread, NT, preferred_element_type=jnp.float32)
        mixes_ref[part] = jnp.where(same, full, 0.0).astype(jnp.bfloat16)
    saves[count].start()
    loads[1].wait()
    for n in range(count):
        loads[2 + n].wait()
        here = slice(n * rows, (n + 1) * rows)
        folded_ref[here] = jnp.dot(
            down_ref[here], tq_ref[...], preferred_element_type=jnp.float32
        ).astype(jnp.bfloat16)
        saves[n].start()
    token_ref[0, 0] = 0
    for copy in saves:
        copy.wait()


def prep(time_mix, w_down, w_query, side=256, parts=2, count=8):
    mixes = jax.ShapeDtypeStruct((parts, side, side), jnp.bfloat16)
    folded = jax.ShapeDtypeStruct((w_down.shape[0], w_query.shape[1]), jnp.bfloat16)
    held = (mixes, folded, time_mix, w_down, w_query)
    return pl.pallas_call(
        prep_kernel,
        out_shape=[mixes, folded, jax.ShapeDtypeStruct((1, 1), jnp.int32)],
        in_specs=[IN_HBM] * 3,
        out_specs=[IN_HBM] * 2 + [IN_SMEM],
        scratch_shapes=[pltpu.VMEM(array.shape, array.dtype) for array in held]
        + [pltpu.SemaphoreType.DMA((count + 2,)), pltpu.SemaphoreType.DMA((count + 1,))],
        compiler_params=params(56),
        cost_estimate=cost(w_down.size * w_query.shape[1], 2 * w_down.size),
        name="prep",
    )(time_mix, w_down, w_query)


def mixer_kernel(step, m_ref, q_ref, mixes_ref, up_ref, folded_ref, tq_ref, out_ref):
    frames, points, width = m_ref.shape
    side = mixes_ref.shape[1]
    repeat = side // frames
    hidden = up_ref.shape[1]
    for j in range(points // repeat):
        here = slice(j * repeat, (j + 1) * repeat)
        query = q_ref[here]
        matched = jnp.concatenate([m_ref[f, here] for f in range(frames)], axis=0)
        tokens = jnp.concatenate(
            [matched, jnp.concatenate([query] * frames, axis=0)], axis=1
        ).astype(jnp.float32)
        power = jnp.mean(tokens * tokens, axis=1, keepdims=True)
        normed = (tokens * lax.rsqrt(power + 1e-06)).astype(jnp.bfloat16)
        section = tokens
        for part in range(mixes_ref.shape[0]):
            section = section + jnp.dot(
                mixes_ref[part], normed, preferred_element_type=jnp.float32
            )
        kept = section.astype(jnp.bfloat16)
        section = kept.astype(jnp.float32)
        power = jnp.mean(section * section, axis=1, keepdims=True)
        inner = (section * lax.rsqrt(power + 1e-06)).astype(jnp.bfloat16)
        acc = jnp.dot(kept, tq_ref[...], preferred_element_type=jnp.float32)
        for h in range(0, hidden, step):
            upper = jnp.dot(inner, up_ref[:, h : h + step], preferred_element_type=jnp.float32)
            upper = jax.nn.gelu(upper).astype(jnp.bfloat16)
            acc = acc + jnp.dot(
                upper, folded_ref[h : h + step], preferred_element_type=jnp.float32
            )
        delta = acc.astype(jnp.bfloat16).astype(jnp.float32)
        query = query.astype(jnp.float32)
        for f in range(frames):
            out_ref[f, here] = (query + delta[f * repeat : (f + 1) * repeat]).astype(jnp.bfloat16)


def mixer(matched, query, mixes, w_up, folded, w_query, step=256):
    return pl.pallas_call(
        functools.partial(mixer_kernel, step),
        out_shape=jax.ShapeDtypeStruct(matched.shape, jnp.bfloat16),
        in_specs=[IN_VMEM] * 6,
        out_specs=IN_VMEM,
        compiler_params=params(16),
        cost_estimate=cost(matched.shape[0] * matched.shape[1] * (w_up.size + folded.size), 2 * w_up.size),
        name="mixer",
    )(matched, query, mixes, w_up, folded, w_query)


def ring_pairs(chips, step):
    return [
        (chip * 2 + core, (chip + step) % chips * 2 + core)
        for chip in range(chips)
        for core in range(2)
    ]


def swap_pairs(chips):
    return [(chip * 2 + core, chip * 2 + 1 - core) for chip in range(chips) for core in range(2)]


def shards(feats, query_frame, query_pos, time_mix, w_up, w_down, w_query):
    points = query_frame.shape[0]
    groups = lax.axis_size("tm")
    share = points // groups
    chips = lax.axis_size("pts") // 2
    width = feats.shape[2]
    tile, want = begin(feats[0], query_frame.reshape(1, points), query_pos.reshape(1, points))
    mixes, folded, token = prep(time_mix, w_down, w_query)
    swap = swap_pairs(chips)
    up, down = ring_pairs(chips, 1), ring_pairs(chips, -1)
    half = chips // 2
    tiles = [tile, lax.ppermute(tile, "pts", swap)]
    aways = [0]
    own = []
    done = 0
    below, above = lax.ppermute(feats[0], "pts", up), lax.ppermute(feats[0], "pts", down)
    for step in range(1, half + 1):
        sent = [above, below] if step < half else [below]
        if step < half:
            below = lax.ppermute(below, "pts", up)
            above = lax.ppermute(above, "pts", down) if step + 1 < half else None
        if step > 1 and step < half:
            after = (token,) if step == 2 else ()
            picked, *sent = pick(want, aways[done:], tiles[2 * done :], own, sent, after)
            own = [picked]
            done = len(aways)
        elif step == half:
            own = pick(want, aways[done:], tiles[2 * done :], own)
            done = len(aways)
        for piece in sent:
            tiles += [piece, lax.ppermute(piece, "pts", swap)]
        aways += [step, -step] if step < half else [-step]
    own = pick(want, aways[done:], tiles[2 * done :], own)
    parts = lax.all_to_all(own[0].reshape(groups, share, width), "tm", 0, 0, tiled=True)
    query_here, copies = join(parts)
    query = lax.all_to_all(copies, "tm", 0, 0, tiled=True).reshape(points, width)
    matched = match(query, tiles).reshape(groups, share, width)
    matched = lax.all_to_all(matched, "tm", 0, 0, tiled=True)
    refined = mixer(matched, query_here, mixes, w_up, folded, w_query)
    refined = lax.all_to_all(refined, "tm", 0, 0, tiled=True).reshape(points, width)
    return rematch(refined, aways, tiles)


def solution(mesh):
    placed = (P("tm", "pts", None), P("pts"), P("pts"), P(), P(), P(), P())
    return jax.shard_map(
        shards,
        mesh=mesh,
        in_specs=placed,
        out_specs=(P("tm", "pts"), P("tm", "pts")),
        check_vma=False,
    )
```

```python
import functools

import jax
import jax.numpy as jnp
from jax import lax
from jax.experimental import pallas as pl
from jax.experimental.pallas import tpu as pltpu
from jax.sharding import PartitionSpec as P

GRID = 64
LOG2E = 1.4426950408889634
IN_VMEM = pl.BlockSpec(memory_space=pltpu.VMEM)
IN_HBM = pl.BlockSpec(memory_space=pltpu.HBM)
NT = (((1,), (1,)), ((), ()))


def params(megabytes):
    return pltpu.CompilerParams(vmem_limit_bytes=megabytes << 20)


def cost(macs, nbytes):
    return pl.CostEstimate(flops=2 * macs, bytes_accessed=nbytes, transcendentals=0)


def tile_bases(aways, rows):
    chips = lax.axis_size("pts") // 2
    place = lax.axis_index("pts")
    core = lax.rem(place, 2)
    bases = []
    for away in aways:
        chip = lax.rem(place // 2 + (away + chips) % chips, chips)
        bases += [(chip * 2 + core) * rows, (chip * 2 + 1 - core) * rows]
    return bases


def begin_kernel(tile_hbm, frame_hbm, pos_hbm, tile_out, want_ref, frame_ref, pos_ref, sems):
    pairs = [(frame_hbm, frame_ref), (pos_hbm, pos_ref), (tile_hbm, tile_out)]
    copies = [
        pltpu.make_async_copy(source, target, sems.at[n]) for n, (source, target) in enumerate(pairs)
    ]
    for copy in copies:
        copy.start()
    copies[0].wait()
    copies[1].wait()
    want = jnp.where(frame_ref[...] == lax.axis_index("tm"), pos_ref[...], -1)
    for first in range(0, want.shape[1], 128):
        row = jnp.broadcast_to(want[:, first : first + 128], (128, 128))
        want_ref[first : first + 128] = jnp.transpose(row)
    copies[2].wait()


def begin(tile, query_frame, query_pos):
    points = query_pos.shape[1]
    return pl.pallas_call(
        begin_kernel,
        out_shape=[
            jax.ShapeDtypeStruct(tile.shape, tile.dtype),
            jax.ShapeDtypeStruct((points, 128), jnp.int32),
        ],
        in_specs=[IN_HBM] * 3,
        out_specs=[IN_VMEM] * 2,
        scratch_shapes=[pltpu.VMEM((1, points), jnp.int32)] * 2 + [pltpu.SemaphoreType.DMA((3,))],
        compiler_params=params(6),
        cost_estimate=cost(points * 128, 4 * points * 128),
        name="begin",
    )(tile, query_frame, query_pos)


def pick_kernel(aways, given, sent, want_ref, *refs):
    count = 2 * len(aways)
    tiles, refs = refs[:count], refs[count:]
    before, refs = refs[:given], refs[given:]
    sources, out, targets = refs[:sent], refs[-1 - sent], refs[len(refs) - sent :]
    want = want_ref[...]
    lane = lax.broadcasted_iota(jnp.int32, (1, 128), 1)
    total = None
    for tile, base in zip(tiles, tile_bases(aways, tiles[0].shape[0])):
        hot = jnp.concatenate(
            [
                (want == lane + (base + first)).astype(jnp.float32).astype(jnp.bfloat16)
                for first in range(0, tile.shape[0], 128)
            ],
            axis=1,
        )
        part = jnp.dot(hot, tile[...], preferred_element_type=jnp.float32)
        total = part if total is None else total + part
    for other in before:
        total = total + other[...].astype(jnp.float32)
    out[...] = total.astype(jnp.bfloat16)
    for source, target in zip(sources, targets):
        target[...] = source[...]


def pick(want, aways, tiles, before=(), sent=()):
    points, width = want.shape[0], tiles[0].shape[1]
    count = len(tiles)
    return pl.pallas_call(
        functools.partial(pick_kernel, aways, len(before), len(sent)),
        out_shape=[jax.ShapeDtypeStruct((points, width), jnp.bfloat16)]
        + [jax.ShapeDtypeStruct(piece.shape, piece.dtype) for piece in sent],
        in_specs=[IN_VMEM] * (1 + count + len(before) + len(sent)),
        out_specs=[IN_VMEM] * (1 + len(sent)),
        compiler_params=params(12),
        cost_estimate=cost(points * count * tiles[0].size, 2 * count * tiles[0].size),
        name="pick",
    )(want, *tiles, *before, *sent)


def join_kernel(parts_ref, query_ref, copies_ref):
    query = jnp.sum(parts_ref[...].astype(jnp.float32), axis=0).astype(jnp.bfloat16)
    query_ref[...] = query
    for n in range(copies_ref.shape[0]):
        copies_ref[n] = query


def join(parts):
    return pl.pallas_call(
        join_kernel,
        out_shape=[
            jax.ShapeDtypeStruct(parts.shape[1:], parts.dtype),
            jax.ShapeDtypeStruct(parts.shape, parts.dtype),
        ],
        in_specs=[IN_VMEM],
        out_specs=[IN_VMEM] * 2,
        compiler_params=params(6),
        cost_estimate=cost(parts.size, 4 * parts.size),
        name="join",
    )(parts)


def match_kernel(count, block, factor, q_ref, *refs):
    tiles, out, bufs = refs[:count], refs[count], refs[count + 1 :]
    rows = tiles[0].shape[0]
    blocks = q_ref.shape[0] // block

    def score(i, t, top):
        s = lax.dot_general(
            q_ref[i * block : (i + 1) * block],
            tiles[t][...],
            NT,
            preferred_element_type=jnp.float32,
        )
        bufs[i % 2][:, t * rows : (t + 1) * rows] = s
        for h in range(0, rows, 128):
            top = s[:, h : h + 128] if top is None else jnp.maximum(top, s[:, h : h + 128])
        return top

    top = None
    for t in range(count):
        top = score(0, t, top)
    for i in range(blocks):
        high = jnp.max(top, axis=1, keepdims=True) * factor
        top = acc = sums = None
        for t in range(count):
            if i + 1 < blocks:
                top = score(i + 1, t, top)
            expo = jnp.exp2(bufs[i % 2][:, t * rows : (t + 1) * rows] * factor - high)
            for h in range(0, rows, 128):
                sums = expo[:, h : h + 128] if sums is None else sums + expo[:, h : h + 128]
            part = jnp.dot(
                expo.astype(jnp.bfloat16), tiles[t][...], preferred_element_type=jnp.float32
            )
            acc = part if acc is None else acc + part
        total = jnp.sum(sums, axis=1, keepdims=True)
        out[i * block : (i + 1) * block] = (acc / total).astype(jnp.bfloat16)


def match(query, tiles, block=256):
    points, width = query.shape
    count = len(tiles)
    places = count * tiles[0].shape[0]
    return pl.pallas_call(
        functools.partial(match_kernel, count, block, LOG2E * width**-0.5),
        out_shape=jax.ShapeDtypeStruct(query.shape, jnp.bfloat16),
        in_specs=[IN_VMEM] * (1 + count),
        out_specs=IN_VMEM,
        scratch_shapes=[pltpu.VMEM((block, places), jnp.float32)] * 2,
        compiler_params=params(18),
        cost_estimate=cost(2 * points * places * width, 2 * places * width),
        name="match",
    )(query, *tiles)


def rematch_kernel(aways, block, factor, q_ref, *refs):
    tiles, out_x, out_y = refs[:-2], refs[-2], refs[-1]
    count = len(tiles)
    rows = tiles[0].shape[0]
    bases = tile_bases(aways, rows)
    sub = lax.broadcasted_iota(jnp.int32, (8, 1), 0)
    columns = [(2 * (sub + at) + 1).astype(jnp.float32) / GRID - 1.0 for at in range(0, GRID, 8)]
    work = [(i, t) for i in range(q_ref.shape[0] // block) for t in range(count)]

    def score(i, t):
        return lax.dot_general(
            tiles[t][...],
            q_ref[i * block : (i + 1) * block],
            NT,
            preferred_element_type=jnp.float32,
        ).reshape(rows // 8, 8, block)

    ahead = score(*work[0])
    for n, (i, t) in enumerate(work):
        s = ahead
        if n + 1 < len(work):
            ahead = score(*work[n + 1])
        if t == 0:
            top = None
            sums = [None] * len(columns)
            sum_y = jnp.zeros((8, block), jnp.float32)
        high = jnp.max(s, axis=0)
        if top is not None:
            high = jnp.maximum(high, top)
            shrink = jnp.exp2((top - high) * factor)
            sum_y = sum_y * shrink
            sums = [value * shrink for value in sums]
        top = high
        high = high * factor
        first = bases[t] // GRID
        for line in range(rows // GRID):
            y = (2 * (first + line) + 1).astype(jnp.float32) / GRID - 1.0
            here = None
            for c in range(len(columns)):
                expo = jnp.exp2(s[line * len(columns) + c] * factor - high)
                sums[c] = expo if sums[c] is None else sums[c] + expo
                here = expo if here is None else here + expo
            sum_y = sum_y + here * y
        if t == count - 1:
            total = sums[0]
            sum_x = sums[0] * columns[0]
            for value, x in zip(sums[1:], columns[1:]):
                total = total + value
                sum_x = sum_x + value * x
            weight = jnp.exp2((top - jnp.max(top, axis=0, keepdims=True)) * factor)
            total = jnp.sum(total * weight, axis=0, keepdims=True)
            here = slice(i * block, (i + 1) * block)
            out_x[:, here] = jnp.sum(sum_x * weight, axis=0, keepdims=True) / total
            out_y[:, here] = jnp.sum(sum_y * weight, axis=0, keepdims=True) / total


def rematch(refined, aways, tiles, block=256):
    points, width = refined.shape
    count = len(tiles)
    places = count * tiles[0].shape[0]
    return pl.pallas_call(
        functools.partial(rematch_kernel, aways, block, LOG2E * width**-0.5),
        out_shape=[jax.ShapeDtypeStruct((1, points), jnp.float32)] * 2,
        in_specs=[IN_VMEM] * (1 + count),
        out_specs=[IN_VMEM] * 2,
        compiler_params=params(12),
        cost_estimate=cost(points * places * width, 2 * places * width),
        name="rematch",
    )(refined, *tiles)


def prep_kernel(mix_ref, down_ref, to_query_ref, mixes_ref, folded_ref):
    frames = mix_ref.shape[0]
    side = mixes_ref.shape[1]
    repeat = side // frames

    def iota(shape, axis):
        return lax.broadcasted_iota(jnp.int32, shape, axis)

    spread = iota((side, frames), 0) // repeat == iota((side, frames), 1)
    spread = spread.astype(jnp.float32).astype(jnp.bfloat16)
    same = iota((side, side), 0) % repeat == iota((side, side), 1) % repeat
    rest = mix_ref[...]
    for part in range(mixes_ref.shape[0]):
        now = rest.astype(jnp.bfloat16)
        rest = rest - now.astype(jnp.float32)
        rows = jnp.dot(spread, now, preferred_element_type=jnp.float32).astype(jnp.bfloat16)
        full = lax.dot_general(rows, spread, NT, preferred_element_type=jnp.float32)
        mixes_ref[part] = jnp.where(same, full, 0.0).astype(jnp.bfloat16)
    folded_ref[...] = jnp.dot(
        down_ref[...], to_query_ref[...], preferred_element_type=jnp.float32
    ).astype(jnp.bfloat16)


def prep(time_mix, w_down, w_query, side=256, parts=2):
    hidden, width = w_down.shape
    return pl.pallas_call(
        prep_kernel,
        out_shape=[
            jax.ShapeDtypeStruct((parts, side, side), jnp.bfloat16),
            jax.ShapeDtypeStruct((hidden, w_query.shape[1]), jnp.bfloat16),
        ],
        in_specs=[IN_VMEM] * 3,
        out_specs=[IN_VMEM] * 2,
        compiler_params=params(10),
        cost_estimate=cost(w_down.size * w_query.shape[1], 2 * w_down.size),
        name="prep",
    )(time_mix, w_down, w_query)


def mixer_kernel(step, m_ref, q_ref, mixes_hbm, up_hbm, folded_hbm, tq_hbm, out_ref, *scratch):
    mixes_ref, up_ref, folded_ref, tq_ref, sems = scratch
    frames, points, width = m_ref.shape
    side = mixes_ref.shape[1]
    repeat = side // frames
    hidden = up_ref.shape[1]
    pairs = [(mixes_hbm, mixes_ref), (tq_hbm, tq_ref)]
    for h in range(0, hidden, step):
        part = pl.ds(h, step)
        pairs.append((up_hbm.at[:, part], up_ref.at[:, part]))
        pairs.append((folded_hbm.at[part], folded_ref.at[part]))
    copies = [
        pltpu.make_async_copy(source, target, sems.at[n]) for n, (source, target) in enumerate(pairs)
    ]
    for copy in copies:
        copy.start()
    for j in range(points // repeat):
        here = slice(j * repeat, (j + 1) * repeat)
        query = q_ref[here]
        matched = jnp.concatenate([m_ref[f, here] for f in range(frames)], axis=0)
        tokens = jnp.concatenate(
            [matched, jnp.concatenate([query] * frames, axis=0)], axis=1
        ).astype(jnp.float32)
        power = jnp.mean(tokens * tokens, axis=1, keepdims=True)
        normed = (tokens * lax.rsqrt(power + 1e-06)).astype(jnp.bfloat16)
        if j == 0:
            copies[0].wait()
        section = tokens
        for part in range(mixes_ref.shape[0]):
            section = section + jnp.dot(
                mixes_ref[part], normed, preferred_element_type=jnp.float32
            )
        kept = section.astype(jnp.bfloat16)
        section = kept.astype(jnp.float32)
        power = jnp.mean(section * section, axis=1, keepdims=True)
        inner = (section * lax.rsqrt(power + 1e-06)).astype(jnp.bfloat16)
        if j == 0:
            copies[1].wait()
        acc = jnp.dot(kept, tq_ref[...], preferred_element_type=jnp.float32)
        for n, h in enumerate(range(0, hidden, step)):
            if j == 0:
                copies[2 + 2 * n].wait()
                copies[3 + 2 * n].wait()
            upper = jnp.dot(inner, up_ref[:, h : h + step], preferred_element_type=jnp.float32)
            upper = jax.nn.gelu(upper).astype(jnp.bfloat16)
            acc = acc + jnp.dot(
                upper, folded_ref[h : h + step], preferred_element_type=jnp.float32
            )
        delta = acc.astype(jnp.bfloat16).astype(jnp.float32)
        query = query.astype(jnp.float32)
        for f in range(frames):
            out_ref[f, here] = (query + delta[f * repeat : (f + 1) * repeat]).astype(jnp.bfloat16)


def mixer(matched, query, mixes, w_up, folded, w_query, step=256):
    held = (mixes, w_up, folded, w_query)
    return pl.pallas_call(
        functools.partial(mixer_kernel, step),
        out_shape=jax.ShapeDtypeStruct(matched.shape, jnp.bfloat16),
        in_specs=[IN_VMEM] * 2 + [IN_HBM] * 4,
        out_specs=IN_VMEM,
        scratch_shapes=[pltpu.VMEM(array.shape, array.dtype) for array in held]
        + [pltpu.SemaphoreType.DMA((2 + 2 * (w_up.shape[1] // step),))],
        compiler_params=params(54),
        cost_estimate=cost(matched.shape[0] * matched.shape[1] * (w_up.size + folded.size), 2 * w_up.size),
        name="mixer",
    )(matched, query, mixes, w_up, folded, w_query)


def ring_pairs(chips, step):
    return [
        (chip * 2 + core, (chip + step) % chips * 2 + core)
        for chip in range(chips)
        for core in range(2)
    ]


def swap_pairs(chips):
    return [(chip * 2 + core, chip * 2 + 1 - core) for chip in range(chips) for core in range(2)]


def shards(feats, query_frame, query_pos, time_mix, w_up, w_down, w_query):
    points = query_frame.shape[0]
    groups = lax.axis_size("tm")
    share = points // groups
    chips = lax.axis_size("pts") // 2
    width = feats.shape[2]
    tile, want = begin(feats[0], query_frame.reshape(1, points), query_pos.reshape(1, points))
    swap = swap_pairs(chips)
    up, down = ring_pairs(chips, 1), ring_pairs(chips, -1)
    half = chips // 2
    tiles = [tile, lax.ppermute(tile, "pts", swap)]
    aways = [0]
    own = []
    done = 0
    below, above = lax.ppermute(feats[0], "pts", up), lax.ppermute(feats[0], "pts", down)
    for step in range(1, half + 1):
        sent = [above, below] if step < half else [below]
        if step < half:
            below = lax.ppermute(below, "pts", up)
            above = lax.ppermute(above, "pts", down) if step + 1 < half else None
        if step == half - 1:
            picked, *sent = pick(want, aways[done:], tiles[2 * done :], own, sent)
            own = [picked]
            done = len(aways)
        elif step == half:
            own = pick(want, aways[done:], tiles[2 * done :], own)
            done = len(aways)
        for piece in sent:
            tiles += [piece, lax.ppermute(piece, "pts", swap)]
        aways += [step, -step] if step < half else [-step]
    own = pick(want, aways[done:], tiles[2 * done :], own)
    parts = lax.all_to_all(own[0].reshape(groups, share, width), "tm", 0, 0, tiled=True)
    query_here, copies = join(parts)
    query = lax.all_to_all(copies, "tm", 0, 0, tiled=True).reshape(points, width)
    mixes, folded = prep(time_mix, w_down, w_query)
    matched = match(query, tiles).reshape(groups, share, width)
    matched = lax.all_to_all(matched, "tm", 0, 0, tiled=True)
    refined = mixer(matched, query_here, mixes, w_up, folded, w_query)
    refined = lax.all_to_all(refined, "tm", 0, 0, tiled=True).reshape(points, width)
    return rematch(refined, aways, tiles)


def solution(mesh):
    placed = (P("tm", "pts", None), P("pts"), P("pts"), P(), P(), P(), P())
    return jax.shard_map(
        shards,
        mesh=mesh,
        in_specs=placed,
        out_specs=(P("tm", "pts"), P("tm", "pts")),
        check_vma=False,
    )
```

```python
import functools

import jax
import jax.numpy as jnp
from jax import lax
from jax.experimental import pallas as pl
from jax.experimental.pallas import tpu as pltpu
from jax.sharding import PartitionSpec as P

GRID = 64
LOG2E = 1.4426950408889634
IN_VMEM = pl.BlockSpec(memory_space=pltpu.VMEM)
IN_SMEM = pl.BlockSpec(memory_space=pltpu.SMEM)
IN_HBM = pl.BlockSpec(memory_space=pltpu.HBM)
NT = (((1,), (1,)), ((), ()))


def params(megabytes):
    return pltpu.CompilerParams(vmem_limit_bytes=megabytes << 20)


def cost(macs, nbytes):
    return pl.CostEstimate(flops=2 * macs, bytes_accessed=nbytes, transcendentals=0)


def tile_bases(aways, rows):
    chips = lax.axis_size("pts") // 2
    place = lax.axis_index("pts")
    core = lax.rem(place, 2)
    bases = []
    for away in aways:
        chip = lax.rem(place // 2 + (away + chips) % chips, chips)
        bases += [(chip * 2 + core) * rows, (chip * 2 + 1 - core) * rows]
    return bases


def begin_kernel(tile_hbm, frame_hbm, pos_hbm, tile_out, want_ref, frame_ref, pos_ref, sems):
    pairs = [(frame_hbm, frame_ref), (pos_hbm, pos_ref), (tile_hbm, tile_out)]
    copies = [
        pltpu.make_async_copy(source, target, sems.at[n]) for n, (source, target) in enumerate(pairs)
    ]
    for copy in copies:
        copy.start()
    copies[0].wait()
    copies[1].wait()
    want = jnp.where(frame_ref[...] == lax.axis_index("tm"), pos_ref[...], -1)
    for first in range(0, want.shape[1], 128):
        row = jnp.broadcast_to(want[:, first : first + 128], (128, 128))
        want_ref[first : first + 128] = jnp.transpose(row)
    copies[2].wait()


def begin(tile, query_frame, query_pos):
    points = query_pos.shape[1]
    return pl.pallas_call(
        begin_kernel,
        out_shape=[
            jax.ShapeDtypeStruct(tile.shape, tile.dtype),
            jax.ShapeDtypeStruct((points, 128), jnp.int32),
        ],
        in_specs=[IN_HBM] * 3,
        out_specs=[IN_VMEM] * 2,
        scratch_shapes=[pltpu.VMEM((1, points), jnp.int32)] * 2 + [pltpu.SemaphoreType.DMA((3,))],
        compiler_params=params(6),
        cost_estimate=cost(points * 128, 4 * points * 128),
        name="begin",
    )(tile, query_frame, query_pos)


def pick_kernel(aways, given, sent, want_ref, *refs):
    count = 2 * len(aways)
    tiles, refs = refs[:count], refs[count:]
    before, refs = refs[:given], refs[given:]
    sources, out, targets = refs[:sent], refs[-1 - sent], refs[len(refs) - sent :]
    want = want_ref[...]
    lane = lax.broadcasted_iota(jnp.int32, (1, 128), 1)
    total = None
    for tile, base in zip(tiles, tile_bases(aways, tiles[0].shape[0])):
        hot = jnp.concatenate(
            [
                (want == lane + (base + first)).astype(jnp.float32).astype(jnp.bfloat16)
                for first in range(0, tile.shape[0], 128)
            ],
            axis=1,
        )
        part = jnp.dot(hot, tile[...], preferred_element_type=jnp.float32)
        total = part if total is None else total + part
    for other in before:
        total = total + other[...].astype(jnp.float32)
    out[...] = total.astype(jnp.bfloat16)
    for source, target in zip(sources, targets):
        target[...] = source[...]


def pick(want, aways, tiles, before=(), sent=(), after=()):
    points, width = want.shape[0], tiles[0].shape[1]
    count = len(tiles)

    def kernel(*refs):
        ahead = 1 + count + len(before) + len(sent)
        pick_kernel(aways, len(before), len(sent), *refs[:ahead], *refs[ahead + len(after) :])

    return pl.pallas_call(
        kernel,
        out_shape=[jax.ShapeDtypeStruct((points, width), jnp.bfloat16)]
        + [jax.ShapeDtypeStruct(piece.shape, piece.dtype) for piece in sent],
        in_specs=[IN_VMEM] * (1 + count + len(before) + len(sent))
        + [IN_SMEM] * len(after),
        out_specs=[IN_VMEM] * (1 + len(sent)),
        compiler_params=params(12),
        cost_estimate=cost(points * count * tiles[0].size, 2 * count * tiles[0].size),
        name="pick",
    )(want, *tiles, *before, *sent, *after)


def join_kernel(parts_ref, query_ref, copies_ref):
    query = jnp.sum(parts_ref[...].astype(jnp.float32), axis=0).astype(jnp.bfloat16)
    query_ref[...] = query
    for n in range(copies_ref.shape[0]):
        copies_ref[n] = query


def join(parts):
    return pl.pallas_call(
        join_kernel,
        out_shape=[
            jax.ShapeDtypeStruct(parts.shape[1:], parts.dtype),
            jax.ShapeDtypeStruct(parts.shape, parts.dtype),
        ],
        in_specs=[IN_VMEM],
        out_specs=[IN_VMEM] * 2,
        compiler_params=params(6),
        cost_estimate=cost(parts.size, 4 * parts.size),
        name="join",
    )(parts)


def match_kernel(count, block, factor, q_ref, *refs):
    tiles, out, bufs = refs[:count], refs[count], refs[count + 1 :]
    rows = tiles[0].shape[0]
    blocks = q_ref.shape[0] // block

    def score(i, t, top):
        s = lax.dot_general(
            q_ref[i * block : (i + 1) * block],
            tiles[t][...],
            NT,
            preferred_element_type=jnp.float32,
        )
        bufs[i % 2][:, t * rows : (t + 1) * rows] = s
        for h in range(0, rows, 128):
            top = s[:, h : h + 128] if top is None else jnp.maximum(top, s[:, h : h + 128])
        return top

    top = None
    for t in range(count):
        top = score(0, t, top)
    for i in range(blocks):
        high = jnp.max(top, axis=1, keepdims=True) * factor
        top = acc = sums = None
        for t in range(count):
            if i + 1 < blocks:
                top = score(i + 1, t, top)
            expo = jnp.exp2(bufs[i % 2][:, t * rows : (t + 1) * rows] * factor - high)
            for h in range(0, rows, 128):
                sums = expo[:, h : h + 128] if sums is None else sums + expo[:, h : h + 128]
            part = jnp.dot(
                expo.astype(jnp.bfloat16), tiles[t][...], preferred_element_type=jnp.float32
            )
            acc = part if acc is None else acc + part
        total = jnp.sum(sums, axis=1, keepdims=True)
        out[i * block : (i + 1) * block] = (acc / total).astype(jnp.bfloat16)


def match(query, tiles, block=256):
    points, width = query.shape
    count = len(tiles)
    places = count * tiles[0].shape[0]
    return pl.pallas_call(
        functools.partial(match_kernel, count, block, LOG2E * width**-0.5),
        out_shape=jax.ShapeDtypeStruct(query.shape, jnp.bfloat16),
        in_specs=[IN_VMEM] * (1 + count),
        out_specs=IN_VMEM,
        scratch_shapes=[pltpu.VMEM((block, places), jnp.float32)] * 2,
        compiler_params=params(18),
        cost_estimate=cost(2 * points * places * width, 2 * places * width),
        name="match",
    )(query, *tiles)


def rematch_kernel(aways, block, factor, q_ref, *refs):
    tiles, out_x, out_y = refs[:-2], refs[-2], refs[-1]
    count = len(tiles)
    rows = tiles[0].shape[0]
    bases = tile_bases(aways, rows)
    sub = lax.broadcasted_iota(jnp.int32, (8, 1), 0)
    columns = [(2 * (sub + at) + 1).astype(jnp.float32) / GRID - 1.0 for at in range(0, GRID, 8)]
    work = [(i, t) for i in range(q_ref.shape[0] // block) for t in range(count)]

    def score(i, t):
        return lax.dot_general(
            tiles[t][...],
            q_ref[i * block : (i + 1) * block],
            NT,
            preferred_element_type=jnp.float32,
        ).reshape(rows // 8, 8, block)

    ahead = score(*work[0])
    for n, (i, t) in enumerate(work):
        s = ahead
        if n + 1 < len(work):
            ahead = score(*work[n + 1])
        if t == 0:
            top = None
            sums = [None] * len(columns)
            sum_y = jnp.zeros((8, block), jnp.float32)
        high = jnp.max(s, axis=0)
        if top is not None:
            high = jnp.maximum(high, top)
            shrink = jnp.exp2((top - high) * factor)
            sum_y = sum_y * shrink
            sums = [value * shrink for value in sums]
        top = high
        high = high * factor
        first = bases[t] // GRID
        for line in range(rows // GRID):
            y = (2 * (first + line) + 1).astype(jnp.float32) / GRID - 1.0
            here = None
            for c in range(len(columns)):
                expo = jnp.exp2(s[line * len(columns) + c] * factor - high)
                sums[c] = expo if sums[c] is None else sums[c] + expo
                here = expo if here is None else here + expo
            sum_y = sum_y + here * y
        if t == count - 1:
            total = sums[0]
            sum_x = sums[0] * columns[0]
            for value, x in zip(sums[1:], columns[1:]):
                total = total + value
                sum_x = sum_x + value * x
            weight = jnp.exp2((top - jnp.max(top, axis=0, keepdims=True)) * factor)
            total = jnp.sum(total * weight, axis=0, keepdims=True)
            here = slice(i * block, (i + 1) * block)
            out_x[:, here] = jnp.sum(sum_x * weight, axis=0, keepdims=True) / total
            out_y[:, here] = jnp.sum(sum_y * weight, axis=0, keepdims=True) / total


def rematch(refined, aways, tiles, block=256):
    points, width = refined.shape
    count = len(tiles)
    places = count * tiles[0].shape[0]
    return pl.pallas_call(
        functools.partial(rematch_kernel, aways, block, LOG2E * width**-0.5),
        out_shape=[jax.ShapeDtypeStruct((1, points), jnp.float32)] * 2,
        in_specs=[IN_VMEM] * (1 + count),
        out_specs=[IN_VMEM] * 2,
        compiler_params=params(12),
        cost_estimate=cost(points * places * width, 2 * places * width),
        name="rematch",
    )(refined, *tiles)


def spread_kernel(mix_ref, mixes_ref, token_ref):
    frames = mix_ref.shape[0]
    side = mixes_ref.shape[1]
    repeat = side // frames

    def iota(shape, axis):
        return lax.broadcasted_iota(jnp.int32, shape, axis)

    spread = iota((side, frames), 0) // repeat == iota((side, frames), 1)
    spread = spread.astype(jnp.float32).astype(jnp.bfloat16)
    same = iota((side, side), 0) % repeat == iota((side, side), 1) % repeat
    rest = mix_ref[...]
    for part in range(mixes_ref.shape[0]):
        now = rest.astype(jnp.bfloat16)
        rest = rest - now.astype(jnp.float32)
        rows = jnp.dot(spread, now, preferred_element_type=jnp.float32).astype(jnp.bfloat16)
        full = lax.dot_general(rows, spread, NT, preferred_element_type=jnp.float32)
        mixes_ref[part] = jnp.where(same, full, 0.0).astype(jnp.bfloat16)
    token_ref[0, 0] = 0


def spread_mix(time_mix, side=256, parts=2):
    return pl.pallas_call(
        spread_kernel,
        out_shape=[
            jax.ShapeDtypeStruct((parts, side, side), jnp.bfloat16),
            jax.ShapeDtypeStruct((1, 1), jnp.int32),
        ],
        in_specs=[IN_VMEM],
        out_specs=[IN_VMEM, IN_SMEM],
        compiler_params=params(6),
        cost_estimate=cost(2 * parts * side * side * 16, parts * side * side * 2),
        name="spread_mix",
    )(time_mix)


def mixer_kernel(step, m_ref, q_ref, mixes_ref, up_ref, down_ref, tq_ref, out_ref, lift_ref):
    frames, points, width = m_ref.shape
    side = mixes_ref.shape[1]
    repeat = side // frames
    hidden = up_ref.shape[1]
    lift_ref[...] = jnp.dot(q_ref[...], up_ref[width:], preferred_element_type=jnp.float32)
    for j in range(points // repeat):
        here = slice(j * repeat, (j + 1) * repeat)
        query = q_ref[here].astype(jnp.float32)
        repeated = jnp.concatenate([query] * frames, axis=0)
        square = jnp.sum(repeated * repeated, axis=1, keepdims=True)
        matched = jnp.concatenate([m_ref[f, here] for f in range(frames)], axis=0)
        matched = matched.astype(jnp.float32)
        power = (jnp.sum(matched * matched, axis=1, keepdims=True) + square) * (0.5 / width)
        scale = lax.rsqrt(power + 1e-06)
        wide = jnp.broadcast_to(scale, (side, 128))
        high = wide.astype(jnp.bfloat16)
        low = (wide - high.astype(jnp.float32)).astype(jnp.bfloat16)
        normed = jnp.concatenate([(matched * scale).astype(jnp.bfloat16), high, low], axis=1)
        blend = jnp.dot(mixes_ref[0], normed, preferred_element_type=jnp.float32)
        for part in range(1, mixes_ref.shape[0]):
            blend = blend + jnp.dot(mixes_ref[part], normed, preferred_element_type=jnp.float32)
        section = (matched + blend[:, :width]).astype(jnp.bfloat16).astype(jnp.float32)
        times = 1.0 + blend[:, width : width + 128] + blend[:, width + 128 :]
        power = (
            jnp.sum(section * section, axis=1, keepdims=True) + times * times * square
        ) * (0.5 / width)
        scale = lax.rsqrt(power + 1e-06)
        inner = (section * jnp.concatenate([scale] * (width // 128), axis=1)).astype(jnp.bfloat16)
        lifted = jnp.concatenate([scale * times] * (step // 128), axis=1)
        lifted = lifted.reshape(frames, repeat, step)
        acc = None
        for h in range(0, hidden, step):
            upper = jnp.dot(
                inner, up_ref[:width, h : h + step], preferred_element_type=jnp.float32
            )
            upper = upper.reshape(frames, repeat, step) + lifted * lift_ref[here, h : h + step][None]
            upper = jax.nn.gelu(upper.reshape(side, step)).astype(jnp.bfloat16)
            part = jnp.dot(upper, down_ref[h : h + step], preferred_element_type=jnp.float32)
            acc = part if acc is None else acc + part
        kept = jnp.concatenate(
            [section, repeated * jnp.concatenate([times] * (width // 128), axis=1)], axis=1
        )
        mixed = (kept + acc).astype(jnp.bfloat16)
        delta = jnp.dot(mixed, tq_ref[...], preferred_element_type=jnp.float32)
        delta = delta.astype(jnp.bfloat16).astype(jnp.float32)
        for f in range(frames):
            out_ref[f, here] = (query + delta[f * repeat : (f + 1) * repeat]).astype(jnp.bfloat16)


def mixer(matched, query, mixes, w_up, w_down, w_query, step=1024):
    tokens = matched.shape[0] * matched.shape[1]
    return pl.pallas_call(
        functools.partial(mixer_kernel, step),
        out_shape=jax.ShapeDtypeStruct(matched.shape, jnp.bfloat16),
        in_specs=[IN_VMEM] * 6,
        out_specs=IN_VMEM,
        scratch_shapes=[pltpu.VMEM((query.shape[0], w_up.shape[1]), jnp.float32)],
        compiler_params=params(18),
        cost_estimate=cost(tokens * (w_up.size + w_down.size), 2 * (w_up.size + w_down.size)),
        name="mixer",
    )(matched, query, mixes, w_up, w_down, w_query)


def ring_pairs(chips, step):
    return [
        (chip * 2 + core, (chip + step) % chips * 2 + core)
        for chip in range(chips)
        for core in range(2)
    ]


def swap_pairs(chips):
    return [(chip * 2 + core, chip * 2 + 1 - core) for chip in range(chips) for core in range(2)]


def shards(feats, query_frame, query_pos, time_mix, w_up, w_down, w_query):
    points = query_frame.shape[0]
    groups = lax.axis_size("tm")
    share = points // groups
    chips = lax.axis_size("pts") // 2
    width = feats.shape[2]
    tile, want = begin(feats[0], query_frame.reshape(1, points), query_pos.reshape(1, points))
    mixes, token = spread_mix(time_mix)
    swap = swap_pairs(chips)
    up, down = ring_pairs(chips, 1), ring_pairs(chips, -1)
    half = chips // 2
    tiles = [tile, lax.ppermute(tile, "pts", swap)]
    aways = [0]
    own = []
    done = 0
    below, above = lax.ppermute(feats[0], "pts", up), lax.ppermute(feats[0], "pts", down)
    for step in range(1, half + 1):
        sent = [above, below] if step < half else [below]
        if step < half:
            below = lax.ppermute(below, "pts", up)
            above = lax.ppermute(above, "pts", down) if step + 1 < half else None
        if step == half - 1:
            picked, *sent = pick(want, aways[done:], tiles[2 * done :], own, sent, (token,))
            own = [picked]
            done = len(aways)
        elif step == half:
            own = pick(want, aways[done:], tiles[2 * done :], own)
            done = len(aways)
        for piece in sent:
            tiles += [piece, lax.ppermute(piece, "pts", swap)]
        aways += [step, -step] if step < half else [-step]
    own = pick(want, aways[done:], tiles[2 * done :], own)
    parts = lax.all_to_all(own[0].reshape(groups, share, width), "tm", 0, 0, tiled=True)
    query_here, copies = join(parts)
    query = lax.all_to_all(copies, "tm", 0, 0, tiled=True).reshape(points, width)
    matched = match(query, tiles).reshape(groups, share, width)
    matched = lax.all_to_all(matched, "tm", 0, 0, tiled=True)
    refined = mixer(matched, query_here, mixes, w_up, w_down, w_query)
    refined = lax.all_to_all(refined, "tm", 0, 0, tiled=True).reshape(points, width)
    return rematch(refined, aways, tiles)


def solution(mesh):
    placed = (P("tm", "pts", None), P("pts"), P("pts"), P(), P(), P(), P())
    return jax.shard_map(
        shards,
        mesh=mesh,
        in_specs=placed,
        out_specs=(P("tm", "pts"), P("tm", "pts")),
        check_vma=False,
    )
```

```python
import functools

import jax
import jax.numpy as jnp
from jax import lax
from jax.experimental import pallas as pl
from jax.experimental.pallas import tpu as pltpu
from jax.sharding import PartitionSpec as P

GRID = 64
LOG2E = 1.4426950408889634
IN_VMEM = pl.BlockSpec(memory_space=pltpu.VMEM)
IN_SMEM = pl.BlockSpec(memory_space=pltpu.SMEM)
IN_HBM = pl.BlockSpec(memory_space=pltpu.HBM)
NT = (((1,), (1,)), ((), ()))


def params(megabytes):
    return pltpu.CompilerParams(vmem_limit_bytes=megabytes << 20)


def cost(macs, nbytes):
    return pl.CostEstimate(flops=2 * macs, bytes_accessed=nbytes, transcendentals=0)


def tile_bases(marks, rows):
    chips = lax.axis_size("pts") // 2
    place = lax.axis_index("pts")
    core = lax.rem(place, 2)
    bases = []
    for away, other in marks:
        chip = lax.rem(place // 2 + (away + chips) % chips, chips)
        bases.append((chip * 2 + (1 - core if other else core)) * rows)
    return bases


def begin_kernel(tile_hbm, frame_hbm, pos_hbm, tile_out, want_ref, frame_ref, pos_ref, sems):
    pairs = [(frame_hbm, frame_ref), (pos_hbm, pos_ref), (tile_hbm, tile_out)]
    copies = [
        pltpu.make_async_copy(source, target, sems.at[n]) for n, (source, target) in enumerate(pairs)
    ]
    for copy in copies:
        copy.start()
    copies[0].wait()
    copies[1].wait()
    want = jnp.where(frame_ref[...] == lax.axis_index("tm"), pos_ref[...], -1)
    for first in range(0, want.shape[1], 128):
        row = jnp.broadcast_to(want[:, first : first + 128], (128, 128))
        want_ref[first : first + 128] = jnp.transpose(row)
    copies[2].wait()


def begin(tile, query_frame, query_pos):
    points = query_pos.shape[1]
    return pl.pallas_call(
        begin_kernel,
        out_shape=[
            jax.ShapeDtypeStruct(tile.shape, tile.dtype),
            jax.ShapeDtypeStruct((points, 128), jnp.int32),
        ],
        in_specs=[IN_HBM] * 3,
        out_specs=[IN_VMEM] * 2,
        scratch_shapes=[pltpu.VMEM((1, points), jnp.int32)] * 2 + [pltpu.SemaphoreType.DMA((3,))],
        compiler_params=params(6),
        cost_estimate=cost(points * 128, 4 * points * 128),
        name="begin",
    )(tile, query_frame, query_pos)


def pick_kernel(marks, given, sent, want_ref, *refs):
    count = len(marks)
    tiles, refs = refs[:count], refs[count:]
    before, refs = refs[:given], refs[given:]
    sources, out, targets = refs[:sent], refs[-1 - sent], refs[len(refs) - sent :]
    want = want_ref[...]
    lane = lax.broadcasted_iota(jnp.int32, (1, 128), 1)
    total = None
    for tile, base in zip(tiles, tile_bases(marks, tiles[0].shape[0])):
        hot = jnp.concatenate(
            [
                (want == lane + (base + first)).astype(jnp.float32).astype(jnp.bfloat16)
                for first in range(0, tile.shape[0], 128)
            ],
            axis=1,
        )
        part = jnp.dot(hot, tile[...], preferred_element_type=jnp.float32)
        total = part if total is None else total + part
    for other in before:
        total = total + other[...].astype(jnp.float32)
    out[...] = total.astype(jnp.bfloat16)
    for source, target in zip(sources, targets):
        target[...] = source[...]


def pick(want, marks, tiles, before=(), sent=(), after=()):
    points, width = want.shape[0], tiles[0].shape[1]
    count = len(tiles)

    def kernel(*refs):
        ahead = 1 + count + len(before) + len(sent)
        pick_kernel(marks, len(before), len(sent), *refs[:ahead], *refs[ahead + len(after) :])

    return pl.pallas_call(
        kernel,
        out_shape=[jax.ShapeDtypeStruct((points, width), jnp.bfloat16)]
        + [jax.ShapeDtypeStruct(piece.shape, piece.dtype) for piece in sent],
        in_specs=[IN_VMEM] * (1 + count + len(before) + len(sent))
        + [IN_SMEM] * len(after),
        out_specs=[IN_VMEM] * (1 + len(sent)),
        compiler_params=params(12),
        cost_estimate=cost(points * count * tiles[0].size, 2 * count * tiles[0].size),
        name="pick",
    )(want, *tiles, *before, *sent, *after)


def join_kernel(parts_ref, query_ref, copies_ref):
    query = jnp.sum(parts_ref[...].astype(jnp.float32), axis=0).astype(jnp.bfloat16)
    query_ref[...] = query
    for n in range(copies_ref.shape[0]):
        copies_ref[n] = query


def join(parts):
    return pl.pallas_call(
        join_kernel,
        out_shape=[
            jax.ShapeDtypeStruct(parts.shape[1:], parts.dtype),
            jax.ShapeDtypeStruct(parts.shape, parts.dtype),
        ],
        in_specs=[IN_VMEM],
        out_specs=[IN_VMEM] * 2,
        compiler_params=params(6),
        cost_estimate=cost(parts.size, 4 * parts.size),
        name="join",
    )(parts)


def match_kernel(count, block, factor, q_ref, *refs):
    tiles, out, bufs = refs[:count], refs[count], refs[count + 1 :]
    rows = tiles[0].shape[0]
    blocks = q_ref.shape[0] // block

    def score(i, t, top):
        s = lax.dot_general(
            q_ref[i * block : (i + 1) * block],
            tiles[t][...],
            NT,
            preferred_element_type=jnp.float32,
        )
        bufs[i % 2][:, t * rows : (t + 1) * rows] = s
        for h in range(0, rows, 128):
            top = s[:, h : h + 128] if top is None else jnp.maximum(top, s[:, h : h + 128])
        return top

    top = None
    for t in range(count):
        top = score(0, t, top)
    for i in range(blocks):
        high = jnp.max(top, axis=1, keepdims=True) * factor
        top = acc = sums = None
        for t in range(count):
            if i + 1 < blocks:
                top = score(i + 1, t, top)
            expo = jnp.exp2(bufs[i % 2][:, t * rows : (t + 1) * rows] * factor - high)
            for h in range(0, rows, 128):
                sums = expo[:, h : h + 128] if sums is None else sums + expo[:, h : h + 128]
            part = jnp.dot(
                expo.astype(jnp.bfloat16), tiles[t][...], preferred_element_type=jnp.float32
            )
            acc = part if acc is None else acc + part
        total = jnp.sum(sums, axis=1, keepdims=True)
        out[i * block : (i + 1) * block] = (acc / total).astype(jnp.bfloat16)


def match(query, tiles, block=256):
    points, width = query.shape
    count = len(tiles)
    places = count * tiles[0].shape[0]
    return pl.pallas_call(
        functools.partial(match_kernel, count, block, LOG2E * width**-0.5),
        out_shape=jax.ShapeDtypeStruct(query.shape, jnp.bfloat16),
        in_specs=[IN_VMEM] * (1 + count),
        out_specs=IN_VMEM,
        scratch_shapes=[pltpu.VMEM((block, places), jnp.float32)] * 2,
        compiler_params=params(18),
        cost_estimate=cost(2 * points * places * width, 2 * places * width),
        name="match",
    )(query, *tiles)


def rematch_kernel(marks, block, factor, q_ref, *refs):
    tiles, out_x, out_y = refs[:-2], refs[-2], refs[-1]
    count = len(tiles)
    rows = tiles[0].shape[0]
    bases = tile_bases(marks, rows)
    sub = lax.broadcasted_iota(jnp.int32, (8, 1), 0)
    columns = [(2 * (sub + at) + 1).astype(jnp.float32) / GRID - 1.0 for at in range(0, GRID, 8)]
    work = [(i, t) for i in range(q_ref.shape[0] // block) for t in range(0, count, 2)]

    def score(i, t):
        return [
            lax.dot_general(
                tile[...],
                q_ref[i * block : (i + 1) * block],
                NT,
                preferred_element_type=jnp.float32,
            ).reshape(rows // 8, 8, block)
            for tile in tiles[t : t + 2]
        ]

    ahead = score(*work[0])
    for n, (i, t) in enumerate(work):
        s = ahead
        if n + 1 < len(work):
            ahead = score(*work[n + 1])
        if t == 0:
            top = None
            sums = [None] * len(columns)
            sum_y = jnp.zeros((8, block), jnp.float32)
        high = jnp.maximum(jnp.max(s[0], axis=0), jnp.max(s[1], axis=0))
        if top is not None:
            high = jnp.maximum(high, top)
            shrink = jnp.exp2((top - high) * factor)
            sum_y = sum_y * shrink
            sums = [value * shrink for value in sums]
        top = high
        high = high * factor
        for piece, base in zip(s, bases[t : t + 2]):
            for line in range(rows // GRID):
                y = (2 * (base // GRID + line) + 1).astype(jnp.float32) / GRID - 1.0
                here = None
                for c in range(len(columns)):
                    expo = jnp.exp2(piece[line * len(columns) + c] * factor - high)
                    sums[c] = expo if sums[c] is None else sums[c] + expo
                    here = expo if here is None else here + expo
                sum_y = sum_y + here * y
        if t == count - 2:
            total = sums[0]
            sum_x = sums[0] * columns[0]
            for value, x in zip(sums[1:], columns[1:]):
                total = total + value
                sum_x = sum_x + value * x
            weight = jnp.exp2((top - jnp.max(top, axis=0, keepdims=True)) * factor)
            total = jnp.sum(total * weight, axis=0, keepdims=True)
            here = slice(i * block, (i + 1) * block)
            out_x[:, here] = jnp.sum(sum_x * weight, axis=0, keepdims=True) / total
            out_y[:, here] = jnp.sum(sum_y * weight, axis=0, keepdims=True) / total


def rematch(refined, marks, tiles, block=256):
    points, width = refined.shape
    count = len(tiles)
    places = count * tiles[0].shape[0]
    return pl.pallas_call(
        functools.partial(rematch_kernel, marks, block, LOG2E * width**-0.5),
        out_shape=[jax.ShapeDtypeStruct((1, points), jnp.float32)] * 2,
        in_specs=[IN_VMEM] * (1 + count),
        out_specs=[IN_VMEM] * 2,
        compiler_params=params(12),
        cost_estimate=cost(points * places * width, 2 * places * width),
        name="rematch",
    )(refined, *tiles)


def spread_kernel(mix_ref, mixes_ref, token_ref):
    frames = mix_ref.shape[0]
    side = mixes_ref.shape[1]
    repeat = side // frames

    def iota(shape, axis):
        return lax.broadcasted_iota(jnp.int32, shape, axis)

    spread = iota((side, frames), 0) // repeat == iota((side, frames), 1)
    spread = spread.astype(jnp.float32).astype(jnp.bfloat16)
    same = iota((side, side), 0) % repeat == iota((side, side), 1) % repeat
    rest = mix_ref[...]
    for part in range(mixes_ref.shape[0]):
        now = rest.astype(jnp.bfloat16)
        rest = rest - now.astype(jnp.float32)
        rows = jnp.dot(spread, now, preferred_element_type=jnp.float32).astype(jnp.bfloat16)
        full = lax.dot_general(rows, spread, NT, preferred_element_type=jnp.float32)
        mixes_ref[part] = jnp.where(same, full, 0.0).astype(jnp.bfloat16)
    token_ref[0, 0] = 0


def spread_mix(time_mix, side=256, parts=2):
    return pl.pallas_call(
        spread_kernel,
        out_shape=[
            jax.ShapeDtypeStruct((parts, side, side), jnp.bfloat16),
            jax.ShapeDtypeStruct((1, 1), jnp.int32),
        ],
        in_specs=[IN_VMEM],
        out_specs=[IN_VMEM, IN_SMEM],
        compiler_params=params(6),
        cost_estimate=cost(2 * parts * side * side * 16, parts * side * side * 2),
        name="spread_mix",
    )(time_mix)


def mixer_kernel(step, m_ref, q_ref, mixes_ref, up_ref, down_ref, tq_ref, out_ref, lift_ref):
    frames, points, width = m_ref.shape
    side = mixes_ref.shape[1]
    repeat = side // frames
    hidden = up_ref.shape[1]
    lift_ref[...] = jnp.dot(q_ref[...], up_ref[width:], preferred_element_type=jnp.float32)
    for j in range(points // repeat):
        here = slice(j * repeat, (j + 1) * repeat)
        query = q_ref[here].astype(jnp.float32)
        repeated = jnp.concatenate([query] * frames, axis=0)
        square = jnp.sum(repeated * repeated, axis=1, keepdims=True)
        matched = jnp.concatenate([m_ref[f, here] for f in range(frames)], axis=0)
        matched = matched.astype(jnp.float32)
        power = (jnp.sum(matched * matched, axis=1, keepdims=True) + square) * (0.5 / width)
        scale = lax.rsqrt(power + 1e-06)
        wide = jnp.broadcast_to(scale, (side, 128))
        high = wide.astype(jnp.bfloat16)
        low = (wide - high.astype(jnp.float32)).astype(jnp.bfloat16)
        normed = jnp.concatenate([(matched * scale).astype(jnp.bfloat16), high, low], axis=1)
        blend = jnp.dot(mixes_ref[0], normed, preferred_element_type=jnp.float32)
        for part in range(1, mixes_ref.shape[0]):
            blend = blend + jnp.dot(mixes_ref[part], normed, preferred_element_type=jnp.float32)
        section = (matched + blend[:, :width]).astype(jnp.bfloat16).astype(jnp.float32)
        times = 1.0 + blend[:, width : width + 128] + blend[:, width + 128 :]
        power = (
            jnp.sum(section * section, axis=1, keepdims=True) + times * times * square
        ) * (0.5 / width)
        scale = lax.rsqrt(power + 1e-06)
        inner = (section * jnp.concatenate([scale] * (width // 128), axis=1)).astype(jnp.bfloat16)
        lifted = jnp.concatenate([scale * times] * (step // 128), axis=1)
        lifted = lifted.reshape(frames, repeat, step)
        acc = None
        for h in range(0, hidden, step):
            upper = jnp.dot(
                inner, up_ref[:width, h : h + step], preferred_element_type=jnp.float32
            )
            upper = upper.reshape(frames, repeat, step) + lifted * lift_ref[here, h : h + step][None]
            upper = jax.nn.gelu(upper.reshape(side, step)).astype(jnp.bfloat16)
            part = jnp.dot(upper, down_ref[h : h + step], preferred_element_type=jnp.float32)
            acc = part if acc is None else acc + part
        kept = jnp.concatenate(
            [section, repeated * jnp.concatenate([times] * (width // 128), axis=1)], axis=1
        )
        mixed = (kept + acc).astype(jnp.bfloat16)
        delta = jnp.dot(mixed, tq_ref[...], preferred_element_type=jnp.float32)
        delta = delta.astype(jnp.bfloat16).astype(jnp.float32)
        for f in range(frames):
            out_ref[f, here] = (query + delta[f * repeat : (f + 1) * repeat]).astype(jnp.bfloat16)


def mixer(matched, query, mixes, w_up, w_down, w_query, step=1024):
    tokens = matched.shape[0] * matched.shape[1]
    return pl.pallas_call(
        functools.partial(mixer_kernel, step),
        out_shape=jax.ShapeDtypeStruct(matched.shape, jnp.bfloat16),
        in_specs=[IN_VMEM] * 6,
        out_specs=IN_VMEM,
        scratch_shapes=[pltpu.VMEM((query.shape[0], w_up.shape[1]), jnp.float32)],
        compiler_params=params(18),
        cost_estimate=cost(tokens * (w_up.size + w_down.size), 2 * (w_up.size + w_down.size)),
        name="mixer",
    )(matched, query, mixes, w_up, w_down, w_query)


def ring_pairs(chips, step):
    return [
        (chip * 2 + core, (chip + step) % chips * 2 + core)
        for chip in range(chips)
        for core in range(2)
    ]


def swap_pairs(chips):
    return [(chip * 2 + core, chip * 2 + 1 - core) for chip in range(chips) for core in range(2)]


def shards(feats, query_frame, query_pos, time_mix, w_up, w_down, w_query):
    points = query_frame.shape[0]
    groups = lax.axis_size("tm")
    share = points // groups
    chips = lax.axis_size("pts") // 2
    width = feats.shape[2]
    tile, want = begin(feats[0], query_frame.reshape(1, points), query_pos.reshape(1, points))
    mixes, token = spread_mix(time_mix)
    swap = swap_pairs(chips)
    up, down = ring_pairs(chips, 1), ring_pairs(chips, -1)
    half = chips // 2
    tiles = []
    marks = []
    own = []
    done = 0

    def hold(piece, away, other):
        tiles.append(piece)
        marks.append((away, other))

    def swapped(piece):
        return lax.ppermute(piece, "pts", swap)

    hold(tile, 0, False)
    hold(swapped(tile), 0, True)
    below, above = lax.ppermute(feats[0], "pts", up), lax.ppermute(feats[0], "pts", down)
    for step in range(1, half):
        arrived = [(above, step), (below, -step)]
        below = lax.ppermute(below, "pts", up)
        if step + 1 < half:
            above = lax.ppermute(above, "pts", down)
        for piece, away in arrived:
            hold(piece, away, False)
        sent = [piece for piece, _ in arrived]
        if step == half - 1:
            picked, *sent = pick(want, marks, tiles, own, sent, (token,))
            own = [picked]
            done = len(tiles)
        for piece, (_, away) in zip(sent, arrived):
            hold(swapped(piece), away, True)
    hold(below, -half, False)
    last = swapped(below)
    own = pick(want, marks[done:], tiles[done:], own)
    hold(last, -half, True)
    own = pick(want, marks[-1:], tiles[-1:], own)
    parts = lax.all_to_all(own[0].reshape(groups, share, width), "tm", 0, 0, tiled=True)
    query_here, copies = join(parts)
    query = lax.all_to_all(copies, "tm", 0, 0, tiled=True).reshape(points, width)
    matched = match(query, tiles).reshape(groups, share, width)
    matched = lax.all_to_all(matched, "tm", 0, 0, tiled=True)
    refined = mixer(matched, query_here, mixes, w_up, w_down, w_query)
    refined = lax.all_to_all(refined, "tm", 0, 0, tiled=True).reshape(points, width)
    return rematch(refined, marks, tiles)


def solution(mesh):
    placed = (P("tm", "pts", None), P("pts"), P("pts"), P(), P(), P(), P())
    return jax.shard_map(
        shards,
        mesh=mesh,
        in_specs=placed,
        out_specs=(P("tm", "pts"), P("tm", "pts")),
        check_vma=False,
    )
```

```python
import functools

import jax
import jax.numpy as jnp
from jax import lax
from jax.experimental import pallas as pl
from jax.experimental.pallas import tpu as pltpu
from jax.sharding import PartitionSpec as P

GRID = 64
LOG2E = 1.4426950408889634
IN_VMEM = pl.BlockSpec(memory_space=pltpu.VMEM)
IN_SMEM = pl.BlockSpec(memory_space=pltpu.SMEM)
IN_HBM = pl.BlockSpec(memory_space=pltpu.HBM)
NT = (((1,), (1,)), ((), ()))


def params(megabytes):
    return pltpu.CompilerParams(vmem_limit_bytes=megabytes << 20)


def cost(macs, nbytes):
    return pl.CostEstimate(flops=2 * macs, bytes_accessed=nbytes, transcendentals=0)


def tile_bases(marks, rows):
    chips = lax.axis_size("pts") // 2
    place = lax.axis_index("pts")
    core = lax.rem(place, 2)
    bases = []
    for away, other in marks:
        chip = lax.rem(place // 2 + (away + chips) % chips, chips)
        bases.append((chip * 2 + (1 - core if other else core)) * rows)
    return bases


def begin_kernel(tile_hbm, frame_hbm, pos_hbm, tile_out, want_ref, frame_ref, pos_ref, sems):
    pairs = [(frame_hbm, frame_ref), (pos_hbm, pos_ref), (tile_hbm, tile_out)]
    copies = [
        pltpu.make_async_copy(source, target, sems.at[n]) for n, (source, target) in enumerate(pairs)
    ]
    for copy in copies:
        copy.start()
    copies[0].wait()
    copies[1].wait()
    want = jnp.where(frame_ref[...] == lax.axis_index("tm"), pos_ref[...], -1)
    for first in range(0, want.shape[1], 128):
        row = jnp.broadcast_to(want[:, first : first + 128], (128, 128))
        want_ref[first : first + 128] = jnp.transpose(row)
    copies[2].wait()


def begin(tile, query_frame, query_pos):
    points = query_pos.shape[1]
    return pl.pallas_call(
        begin_kernel,
        out_shape=[
            jax.ShapeDtypeStruct(tile.shape, tile.dtype),
            jax.ShapeDtypeStruct((points, 128), jnp.int32),
        ],
        in_specs=[IN_HBM] * 3,
        out_specs=[IN_VMEM] * 2,
        scratch_shapes=[pltpu.VMEM((1, points), jnp.int32)] * 2 + [pltpu.SemaphoreType.DMA((3,))],
        compiler_params=params(6),
        cost_estimate=cost(points * 128, 4 * points * 128),
        name="begin",
    )(tile, query_frame, query_pos)


def pick_kernel(marks, given, sent, want_ref, *refs):
    count = len(marks)
    tiles, refs = refs[:count], refs[count:]
    before, refs = refs[:given], refs[given:]
    sources, out, targets = refs[:sent], refs[-1 - sent], refs[len(refs) - sent :]
    want = want_ref[...]
    lane = lax.broadcasted_iota(jnp.int32, (1, 128), 1)
    total = None
    for tile, base in zip(tiles, tile_bases(marks, tiles[0].shape[0])):
        hot = jnp.concatenate(
            [
                (want == lane + (base + first)).astype(jnp.float32).astype(jnp.bfloat16)
                for first in range(0, tile.shape[0], 128)
            ],
            axis=1,
        )
        part = jnp.dot(hot, tile[...], preferred_element_type=jnp.float32)
        total = part if total is None else total + part
    for other in before:
        total = total + other[...].astype(jnp.float32)
    out[...] = total.astype(jnp.bfloat16)
    for source, target in zip(sources, targets):
        target[...] = source[...]


def pick(want, marks, tiles, before=(), sent=(), after=()):
    points, width = want.shape[0], tiles[0].shape[1]
    count = len(tiles)

    def kernel(*refs):
        ahead = 1 + count + len(before) + len(sent)
        pick_kernel(marks, len(before), len(sent), *refs[:ahead], *refs[ahead + len(after) :])

    return pl.pallas_call(
        kernel,
        out_shape=[jax.ShapeDtypeStruct((points, width), jnp.bfloat16)]
        + [jax.ShapeDtypeStruct(piece.shape, piece.dtype) for piece in sent],
        in_specs=[IN_VMEM] * (1 + count + len(before) + len(sent))
        + [IN_SMEM] * len(after),
        out_specs=[IN_VMEM] * (1 + len(sent)),
        compiler_params=params(12),
        cost_estimate=cost(points * count * tiles[0].size, 2 * count * tiles[0].size),
        name="pick",
    )(want, *tiles, *before, *sent, *after)


def join_kernel(parts_ref, query_ref, copies_ref):
    query = jnp.sum(parts_ref[...].astype(jnp.float32), axis=0).astype(jnp.bfloat16)
    query_ref[...] = query
    for n in range(copies_ref.shape[0]):
        copies_ref[n] = query


def join(parts):
    return pl.pallas_call(
        join_kernel,
        out_shape=[
            jax.ShapeDtypeStruct(parts.shape[1:], parts.dtype),
            jax.ShapeDtypeStruct(parts.shape, parts.dtype),
        ],
        in_specs=[IN_VMEM],
        out_specs=[IN_VMEM] * 2,
        compiler_params=params(6),
        cost_estimate=cost(parts.size, 4 * parts.size),
        name="join",
    )(parts)


def match_kernel(count, block, factor, q_ref, *refs):
    tiles, out, bufs = refs[:count], refs[count], refs[count + 1 :]
    rows = tiles[0].shape[0]
    blocks = q_ref.shape[0] // block

    def score(i, t, top):
        s = lax.dot_general(
            q_ref[i * block : (i + 1) * block],
            tiles[t][...],
            NT,
            preferred_element_type=jnp.float32,
        )
        bufs[i % 2][:, t * rows : (t + 1) * rows] = s
        for h in range(0, rows, 128):
            top = s[:, h : h + 128] if top is None else jnp.maximum(top, s[:, h : h + 128])
        return top

    top = None
    for t in range(count):
        top = score(0, t, top)
    for i in range(blocks):
        high = jnp.max(top, axis=1, keepdims=True) * factor
        top = acc = sums = None
        for t in range(count):
            if i + 1 < blocks:
                top = score(i + 1, t, top)
            expo = jnp.exp2(bufs[i % 2][:, t * rows : (t + 1) * rows] * factor - high)
            for h in range(0, rows, 128):
                sums = expo[:, h : h + 128] if sums is None else sums + expo[:, h : h + 128]
            part = jnp.dot(
                expo.astype(jnp.bfloat16), tiles[t][...], preferred_element_type=jnp.float32
            )
            acc = part if acc is None else acc + part
        total = jnp.sum(sums, axis=1, keepdims=True)
        out[i * block : (i + 1) * block] = (acc / total).astype(jnp.bfloat16)


def match(query, tiles, block=256):
    points, width = query.shape
    count = len(tiles)
    places = count * tiles[0].shape[0]
    return pl.pallas_call(
        functools.partial(match_kernel, count, block, LOG2E * width**-0.5),
        out_shape=jax.ShapeDtypeStruct(query.shape, jnp.bfloat16),
        in_specs=[IN_VMEM] * (1 + count),
        out_specs=IN_VMEM,
        scratch_shapes=[pltpu.VMEM((block, places), jnp.float32)] * 2,
        compiler_params=params(18),
        cost_estimate=cost(2 * points * places * width, 2 * places * width),
        name="match",
    )(query, *tiles)


def rematch_kernel(marks, block, factor, q_ref, *refs):
    tiles, out_x, out_y = refs[:-2], refs[-2], refs[-1]
    count = len(tiles)
    rows = tiles[0].shape[0]
    bases = tile_bases(marks, rows)
    sub = lax.broadcasted_iota(jnp.int32, (8, 1), 0)
    columns = [(2 * (sub + at) + 1).astype(jnp.float32) / GRID - 1.0 for at in range(0, GRID, 8)]
    work = [(i, t) for i in range(q_ref.shape[0] // block) for t in range(0, count, 2)]

    def score(i, t):
        return [
            lax.dot_general(
                tile[...],
                q_ref[i * block : (i + 1) * block],
                NT,
                preferred_element_type=jnp.float32,
            ).reshape(rows // 8, 8, block)
            for tile in tiles[t : t + 2]
        ]

    ahead = score(*work[0])
    for n, (i, t) in enumerate(work):
        s = ahead
        if n + 1 < len(work):
            ahead = score(*work[n + 1])
        if t == 0:
            top = None
            sums = [None] * len(columns)
            sum_y = jnp.zeros((8, block), jnp.float32)
        high = jnp.maximum(jnp.max(s[0], axis=0), jnp.max(s[1], axis=0))
        if top is not None:
            high = jnp.maximum(high, top)
            shrink = jnp.exp2((top - high) * factor)
            sum_y = sum_y * shrink
            sums = [value * shrink for value in sums]
        top = high
        high = high * factor
        for piece, base in zip(s, bases[t : t + 2]):
            for line in range(rows // GRID):
                y = (2 * (base // GRID + line) + 1).astype(jnp.float32) / GRID - 1.0
                here = None
                for c in range(len(columns)):
                    expo = jnp.exp2(piece[line * len(columns) + c] * factor - high)
                    sums[c] = expo if sums[c] is None else sums[c] + expo
                    here = expo if here is None else here + expo
                sum_y = sum_y + here * y
        if t == count - 2:
            total = sums[0]
            sum_x = sums[0] * columns[0]
            for value, x in zip(sums[1:], columns[1:]):
                total = total + value
                sum_x = sum_x + value * x
            weight = jnp.exp2((top - jnp.max(top, axis=0, keepdims=True)) * factor)
            total = jnp.sum(total * weight, axis=0, keepdims=True)
            here = slice(i * block, (i + 1) * block)
            out_x[:, here] = jnp.sum(sum_x * weight, axis=0, keepdims=True) / total
            out_y[:, here] = jnp.sum(sum_y * weight, axis=0, keepdims=True) / total


def rematch(refined, marks, tiles, block=256):
    points, width = refined.shape
    count = len(tiles)
    places = count * tiles[0].shape[0]
    return pl.pallas_call(
        functools.partial(rematch_kernel, marks, block, LOG2E * width**-0.5),
        out_shape=[jax.ShapeDtypeStruct((1, points), jnp.float32)] * 2,
        in_specs=[IN_VMEM] * (1 + count),
        out_specs=[IN_VMEM] * 2,
        compiler_params=params(12),
        cost_estimate=cost(points * places * width, 2 * places * width),
        name="rematch",
    )(refined, *tiles)


def spread_kernel(mix_ref, mixes_ref, token_ref):
    frames = mix_ref.shape[0]
    side = mixes_ref.shape[1]
    repeat = side // frames

    def iota(shape, axis):
        return lax.broadcasted_iota(jnp.int32, shape, axis)

    spread = iota((side, frames), 0) // repeat == iota((side, frames), 1)
    spread = spread.astype(jnp.float32).astype(jnp.bfloat16)
    same = iota((side, side), 0) % repeat == iota((side, side), 1) % repeat
    rest = mix_ref[...]
    for part in range(mixes_ref.shape[0]):
        now = rest.astype(jnp.bfloat16)
        rest = rest - now.astype(jnp.float32)
        rows = jnp.dot(spread, now, preferred_element_type=jnp.float32).astype(jnp.bfloat16)
        full = lax.dot_general(rows, spread, NT, preferred_element_type=jnp.float32)
        mixes_ref[part] = jnp.where(same, full, 0.0).astype(jnp.bfloat16)
    token_ref[0, 0] = 0


def spread_mix(time_mix, side=256, parts=1):
    return pl.pallas_call(
        spread_kernel,
        out_shape=[
            jax.ShapeDtypeStruct((parts, side, side), jnp.bfloat16),
            jax.ShapeDtypeStruct((1, 1), jnp.int32),
        ],
        in_specs=[IN_VMEM],
        out_specs=[IN_VMEM, IN_SMEM],
        compiler_params=params(6),
        cost_estimate=cost(2 * parts * side * side * 16, parts * side * side * 2),
        name="spread_mix",
    )(time_mix)


def mixer_kernel(step, m_ref, q_ref, mixes_ref, up_ref, down_ref, tq_ref, out_ref, lift_ref):
    frames, points, width = m_ref.shape
    side = mixes_ref.shape[1]
    repeat = side // frames
    hidden = up_ref.shape[1]
    lift_ref[...] = jnp.dot(q_ref[...], up_ref[width:], preferred_element_type=jnp.float32)
    for j in range(points // repeat):
        here = slice(j * repeat, (j + 1) * repeat)
        query = q_ref[here].astype(jnp.float32)
        repeated = jnp.concatenate([query] * frames, axis=0)
        square = jnp.sum(repeated * repeated, axis=1, keepdims=True)
        matched = jnp.concatenate([m_ref[f, here] for f in range(frames)], axis=0)
        matched = matched.astype(jnp.float32)
        power = (jnp.sum(matched * matched, axis=1, keepdims=True) + square) * (0.5 / width)
        scale = lax.rsqrt(power + 1e-06)
        wide = jnp.broadcast_to(scale, (side, 128))
        high = wide.astype(jnp.bfloat16)
        low = (wide - high.astype(jnp.float32)).astype(jnp.bfloat16)
        normed = jnp.concatenate([(matched * scale).astype(jnp.bfloat16), high, low], axis=1)
        blend = jnp.dot(mixes_ref[0], normed, preferred_element_type=jnp.float32)
        for part in range(1, mixes_ref.shape[0]):
            blend = blend + jnp.dot(mixes_ref[part], normed, preferred_element_type=jnp.float32)
        section = (matched + blend[:, :width]).astype(jnp.bfloat16).astype(jnp.float32)
        times = 1.0 + blend[:, width : width + 128] + blend[:, width + 128 :]
        power = (
            jnp.sum(section * section, axis=1, keepdims=True) + times * times * square
        ) * (0.5 / width)
        scale = lax.rsqrt(power + 1e-06)
        inner = (section * jnp.concatenate([scale] * (width // 128), axis=1)).astype(jnp.bfloat16)
        lifted = jnp.concatenate([scale * times] * (step // 128), axis=1)
        lifted = lifted.reshape(frames, repeat, step)
        acc = None
        for h in range(0, hidden, step):
            upper = jnp.dot(
                inner, up_ref[:width, h : h + step], preferred_element_type=jnp.float32
            )
            upper = upper.reshape(frames, repeat, step) + lifted * lift_ref[here, h : h + step][None]
            upper = jax.nn.gelu(upper.reshape(side, step)).astype(jnp.bfloat16)
            part = jnp.dot(upper, down_ref[h : h + step], preferred_element_type=jnp.float32)
            acc = part if acc is None else acc + part
        kept = jnp.concatenate(
            [section, repeated * jnp.concatenate([times] * (width // 128), axis=1)], axis=1
        )
        mixed = (kept + acc).astype(jnp.bfloat16)
        delta = jnp.dot(mixed, tq_ref[...], preferred_element_type=jnp.float32)
        delta = delta.astype(jnp.bfloat16).astype(jnp.float32)
        for f in range(frames):
            out_ref[f, here] = (query + delta[f * repeat : (f + 1) * repeat]).astype(jnp.bfloat16)


def mixer(matched, query, mixes, w_up, w_down, w_query, step=1024):
    tokens = matched.shape[0] * matched.shape[1]
    return pl.pallas_call(
        functools.partial(mixer_kernel, step),
        out_shape=jax.ShapeDtypeStruct(matched.shape, jnp.bfloat16),
        in_specs=[IN_VMEM] * 6,
        out_specs=IN_VMEM,
        scratch_shapes=[pltpu.VMEM((query.shape[0], w_up.shape[1]), jnp.float32)],
        compiler_params=params(18),
        cost_estimate=cost(tokens * (w_up.size + w_down.size), 2 * (w_up.size + w_down.size)),
        name="mixer",
    )(matched, query, mixes, w_up, w_down, w_query)


def ring_pairs(chips, step):
    return [
        (chip * 2 + core, (chip + step) % chips * 2 + core)
        for chip in range(chips)
        for core in range(2)
    ]


def swap_pairs(chips):
    return [(chip * 2 + core, chip * 2 + 1 - core) for chip in range(chips) for core in range(2)]


def shards(feats, query_frame, query_pos, time_mix, w_up, w_down, w_query):
    points = query_frame.shape[0]
    groups = lax.axis_size("tm")
    share = points // groups
    chips = lax.axis_size("pts") // 2
    width = feats.shape[2]
    tile, want = begin(feats[0], query_frame.reshape(1, points), query_pos.reshape(1, points))
    mixes, token = spread_mix(time_mix)
    swap = swap_pairs(chips)
    up, down = ring_pairs(chips, 1), ring_pairs(chips, -1)
    half = chips // 2
    tiles = []
    marks = []
    own = []
    done = 0

    def hold(piece, away, other):
        tiles.append(piece)
        marks.append((away, other))

    def swapped(piece):
        return lax.ppermute(piece, "pts", swap)

    hold(tile, 0, False)
    hold(swapped(tile), 0, True)
    below, above = lax.ppermute(feats[0], "pts", up), lax.ppermute(feats[0], "pts", down)
    for step in range(1, half):
        arrived = [(above, step), (below, -step)]
        below = lax.ppermute(below, "pts", up)
        if step + 1 < half:
            above = lax.ppermute(above, "pts", down)
        for piece, away in arrived:
            hold(piece, away, False)
        sent = [piece for piece, _ in arrived]
        if step == half - 1:
            picked, *sent = pick(want, marks, tiles, own, sent, (token,))
            own = [picked]
            done = len(tiles)
        for piece, (_, away) in zip(sent, arrived):
            hold(swapped(piece), away, True)
    hold(below, -half, False)
    last = swapped(below)
    own = pick(want, marks[done:], tiles[done:], own)
    hold(last, -half, True)
    own = pick(want, marks[-1:], tiles[-1:], own)
    parts = lax.all_to_all(own[0].reshape(groups, share, width), "tm", 0, 0, tiled=True)
    query_here, copies = join(parts)
    query = lax.all_to_all(copies, "tm", 0, 0, tiled=True).reshape(points, width)
    matched = match(query, tiles).reshape(groups, share, width)
    matched = lax.all_to_all(matched, "tm", 0, 0, tiled=True)
    refined = mixer(matched, query_here, mixes, w_up, w_down, w_query)
    refined = lax.all_to_all(refined, "tm", 0, 0, tiled=True).reshape(points, width)
    return rematch(refined, marks, tiles)


def solution(mesh):
    placed = (P("tm", "pts", None), P("pts"), P("pts"), P(), P(), P(), P())
    return jax.shard_map(
        shards,
        mesh=mesh,
        in_specs=placed,
        out_specs=(P("tm", "pts"), P("tm", "pts")),
        check_vma=False,
    )
```

```python
import functools

import jax
import jax.numpy as jnp
from jax import lax
from jax.experimental import pallas as pl
from jax.experimental.pallas import tpu as pltpu
from jax.sharding import PartitionSpec as P

GRID = 64
LOG2E = 1.4426950408889634
IN_VMEM = pl.BlockSpec(memory_space=pltpu.VMEM)
IN_SMEM = pl.BlockSpec(memory_space=pltpu.SMEM)
IN_HBM = pl.BlockSpec(memory_space=pltpu.HBM)
NT = (((1,), (1,)), ((), ()))


def params(megabytes):
    return pltpu.CompilerParams(vmem_limit_bytes=megabytes << 20)


def cost(macs, nbytes):
    return pl.CostEstimate(flops=2 * macs, bytes_accessed=nbytes, transcendentals=0)


def tile_bases(marks, rows):
    chips = lax.axis_size("pts") // 2
    place = lax.axis_index("pts")
    core = lax.rem(place, 2)
    bases = []
    for away, other in marks:
        chip = lax.rem(place // 2 + (away + chips) % chips, chips)
        bases.append((chip * 2 + (1 - core if other else core)) * rows)
    return bases


def begin_kernel(tile_hbm, frame_hbm, pos_hbm, tile_out, want_ref, frame_ref, pos_ref, sems):
    pairs = [(frame_hbm, frame_ref), (pos_hbm, pos_ref), (tile_hbm, tile_out)]
    copies = [
        pltpu.make_async_copy(source, target, sems.at[n]) for n, (source, target) in enumerate(pairs)
    ]
    for copy in copies:
        copy.start()
    copies[0].wait()
    copies[1].wait()
    want = jnp.where(frame_ref[...] == lax.axis_index("tm"), pos_ref[...], -1)
    for first in range(0, want.shape[1], 128):
        row = jnp.broadcast_to(want[:, first : first + 128], (128, 128))
        want_ref[first : first + 128] = jnp.transpose(row)
    copies[2].wait()


def begin(tile, query_frame, query_pos):
    points = query_pos.shape[1]
    return pl.pallas_call(
        begin_kernel,
        out_shape=[
            jax.ShapeDtypeStruct(tile.shape, tile.dtype),
            jax.ShapeDtypeStruct((points, 128), jnp.int32),
        ],
        in_specs=[IN_HBM] * 3,
        out_specs=[IN_VMEM] * 2,
        scratch_shapes=[pltpu.VMEM((1, points), jnp.int32)] * 2 + [pltpu.SemaphoreType.DMA((3,))],
        compiler_params=params(6),
        cost_estimate=cost(points * 128, 4 * points * 128),
        name="begin",
    )(tile, query_frame, query_pos)


def pick_kernel(marks, given, sent, want_ref, *refs):
    count = len(marks)
    tiles, refs = refs[:count], refs[count:]
    before, refs = refs[:given], refs[given:]
    sources, out, targets = refs[:sent], refs[-1 - sent], refs[len(refs) - sent :]
    want = want_ref[...]
    lane = lax.broadcasted_iota(jnp.int32, (1, 128), 1)
    total = None
    for tile, base in zip(tiles, tile_bases(marks, tiles[0].shape[0])):
        hot = jnp.concatenate(
            [
                (want == lane + (base + first)).astype(jnp.float32).astype(jnp.bfloat16)
                for first in range(0, tile.shape[0], 128)
            ],
            axis=1,
        )
        part = jnp.dot(hot, tile[...], preferred_element_type=jnp.float32)
        total = part if total is None else total + part
    for other in before:
        total = total + other[...].astype(jnp.float32)
    out[...] = total.astype(jnp.bfloat16)
    for source, target in zip(sources, targets):
        target[...] = source[...]


def pick(want, marks, tiles, before=(), sent=(), after=()):
    points, width = want.shape[0], tiles[0].shape[1]
    count = len(tiles)

    def kernel(*refs):
        ahead = 1 + count + len(before) + len(sent)
        pick_kernel(marks, len(before), len(sent), *refs[:ahead], *refs[ahead + len(after) :])

    return pl.pallas_call(
        kernel,
        out_shape=[jax.ShapeDtypeStruct((points, width), jnp.bfloat16)]
        + [jax.ShapeDtypeStruct(piece.shape, piece.dtype) for piece in sent],
        in_specs=[IN_VMEM] * (1 + count + len(before) + len(sent))
        + [IN_SMEM] * len(after),
        out_specs=[IN_VMEM] * (1 + len(sent)),
        compiler_params=params(12),
        cost_estimate=cost(points * count * tiles[0].size, 2 * count * tiles[0].size),
        name="pick",
    )(want, *tiles, *before, *sent, *after)


def join_kernel(parts_ref, query_ref, copies_ref):
    query = jnp.sum(parts_ref[...].astype(jnp.float32), axis=0).astype(jnp.bfloat16)
    query_ref[...] = query
    for n in range(copies_ref.shape[0]):
        copies_ref[n] = query


def join(parts):
    return pl.pallas_call(
        join_kernel,
        out_shape=[
            jax.ShapeDtypeStruct(parts.shape[1:], parts.dtype),
            jax.ShapeDtypeStruct(parts.shape, parts.dtype),
        ],
        in_specs=[IN_VMEM],
        out_specs=[IN_VMEM] * 2,
        compiler_params=params(6),
        cost_estimate=cost(parts.size, 4 * parts.size),
        name="join",
    )(parts)


def match_kernel(count, block, factor, q_ref, *refs):
    tiles, out, bufs = refs[:count], refs[count], refs[count + 1 :]
    rows = tiles[0].shape[0]
    blocks = q_ref.shape[0] // block

    def score(i, t, top):
        s = lax.dot_general(
            q_ref[i * block : (i + 1) * block],
            tiles[t][...],
            NT,
            preferred_element_type=jnp.float32,
        )
        bufs[i % 2][:, t * rows : (t + 1) * rows] = s
        for h in range(0, rows, 128):
            top = s[:, h : h + 128] if top is None else jnp.maximum(top, s[:, h : h + 128])
        return top

    top = None
    for t in range(count):
        top = score(0, t, top)
    for i in range(blocks):
        high = jnp.max(top, axis=1, keepdims=True) * factor
        top = acc = sums = None
        for t in range(count):
            if i + 1 < blocks:
                top = score(i + 1, t, top)
            expo = jnp.exp2(bufs[i % 2][:, t * rows : (t + 1) * rows] * factor - high)
            for h in range(0, rows, 128):
                sums = expo[:, h : h + 128] if sums is None else sums + expo[:, h : h + 128]
            part = jnp.dot(
                expo.astype(jnp.bfloat16), tiles[t][...], preferred_element_type=jnp.float32
            )
            acc = part if acc is None else acc + part
        total = jnp.sum(sums, axis=1, keepdims=True)
        out[i * block : (i + 1) * block] = (acc / total).astype(jnp.bfloat16)


def match(query, tiles, block=256):
    points, width = query.shape
    count = len(tiles)
    places = count * tiles[0].shape[0]
    return pl.pallas_call(
        functools.partial(match_kernel, count, block, LOG2E * width**-0.5),
        out_shape=jax.ShapeDtypeStruct(query.shape, jnp.bfloat16),
        in_specs=[IN_VMEM] * (1 + count),
        out_specs=IN_VMEM,
        scratch_shapes=[pltpu.VMEM((block, places), jnp.float32)] * 2,
        compiler_params=params(18),
        cost_estimate=cost(2 * points * places * width, 2 * places * width),
        name="match",
    )(query, *tiles)


def rematch_kernel(marks, block, factor, q_ref, *refs):
    tiles, out_x, out_y = refs[:-2], refs[-2], refs[-1]
    count = len(tiles)
    rows = tiles[0].shape[0]
    bases = tile_bases(marks, rows)
    sub = lax.broadcasted_iota(jnp.int32, (8, 1), 0)
    columns = [(2 * (sub + at) + 1).astype(jnp.float32) / GRID - 1.0 for at in range(0, GRID, 8)]
    work = [(i, t) for i in range(q_ref.shape[0] // block) for t in range(0, count, 2)]

    def score(i, t):
        return [
            lax.dot_general(
                tile[...],
                q_ref[i * block : (i + 1) * block],
                NT,
                preferred_element_type=jnp.float32,
            ).reshape(rows // 8, 8, block)
            for tile in tiles[t : t + 2]
        ]

    ahead = score(*work[0])
    for n, (i, t) in enumerate(work):
        s = ahead
        if n + 1 < len(work):
            ahead = score(*work[n + 1])
        if t == 0:
            top = None
            sums = [None] * len(columns)
            sum_y = jnp.zeros((8, block), jnp.float32)
        high = jnp.maximum(jnp.max(s[0], axis=0), jnp.max(s[1], axis=0))
        if top is not None:
            high = jnp.maximum(high, top)
            shrink = jnp.exp2((top - high) * factor)
            sum_y = sum_y * shrink
            sums = [value * shrink for value in sums]
        top = high
        high = high * factor
        for piece, base in zip(s, bases[t : t + 2]):
            for line in range(rows // GRID):
                y = (2 * (base // GRID + line) + 1).astype(jnp.float32) / GRID - 1.0
                here = None
                for c in range(len(columns)):
                    expo = jnp.exp2(piece[line * len(columns) + c] * factor - high)
                    sums[c] = expo if sums[c] is None else sums[c] + expo
                    here = expo if here is None else here + expo
                sum_y = sum_y + here * y
        if t == count - 2:
            total = sums[0]
            sum_x = sums[0] * columns[0]
            for value, x in zip(sums[1:], columns[1:]):
                total = total + value
                sum_x = sum_x + value * x
            weight = jnp.exp2((top - jnp.max(top, axis=0, keepdims=True)) * factor)
            total = jnp.sum(total * weight, axis=0, keepdims=True)
            here = slice(i * block, (i + 1) * block)
            out_x[:, here] = jnp.sum(sum_x * weight, axis=0, keepdims=True) / total
            out_y[:, here] = jnp.sum(sum_y * weight, axis=0, keepdims=True) / total


def rematch(refined, marks, tiles, block=256):
    points, width = refined.shape
    count = len(tiles)
    places = count * tiles[0].shape[0]
    return pl.pallas_call(
        functools.partial(rematch_kernel, marks, block, LOG2E * width**-0.5),
        out_shape=[jax.ShapeDtypeStruct((1, points), jnp.float32)] * 2,
        in_specs=[IN_VMEM] * (1 + count),
        out_specs=[IN_VMEM] * 2,
        compiler_params=params(12),
        cost_estimate=cost(points * places * width, 2 * places * width),
        name="rematch",
    )(refined, *tiles)


def spread_kernel(mix_ref, mixes_ref, token_ref):
    frames = mix_ref.shape[0]
    side = mixes_ref.shape[1]
    repeat = side // frames

    def iota(shape, axis):
        return lax.broadcasted_iota(jnp.int32, shape, axis)

    spread = iota((side, frames), 0) // repeat == iota((side, frames), 1)
    spread = spread.astype(jnp.float32).astype(jnp.bfloat16)
    same = iota((side, side), 0) % repeat == iota((side, side), 1) % repeat
    rest = mix_ref[...]
    for part in range(mixes_ref.shape[0]):
        now = rest.astype(jnp.bfloat16)
        rest = rest - now.astype(jnp.float32)
        rows = jnp.dot(spread, now, preferred_element_type=jnp.float32).astype(jnp.bfloat16)
        full = lax.dot_general(rows, spread, NT, preferred_element_type=jnp.float32)
        mixes_ref[part] = jnp.where(same, full, 0.0).astype(jnp.bfloat16)
    token_ref[0, 0] = 0


def spread_mix(time_mix, side=256, parts=1):
    return pl.pallas_call(
        spread_kernel,
        out_shape=[
            jax.ShapeDtypeStruct((parts, side, side), jnp.bfloat16),
            jax.ShapeDtypeStruct((1, 1), jnp.int32),
        ],
        in_specs=[IN_VMEM],
        out_specs=[IN_VMEM, IN_SMEM],
        compiler_params=params(6),
        cost_estimate=cost(2 * parts * side * side * 16, parts * side * side * 2),
        name="spread_mix",
    )(time_mix)


def mixer_kernel(step, m_ref, q_ref, mixes_ref, up_ref, down_ref, tq_ref, out_ref, lift_ref):
    frames, points, width = m_ref.shape
    side = mixes_ref.shape[1]
    repeat = side // frames
    hidden = up_ref.shape[1]
    lift_ref[...] = jnp.dot(q_ref[...], up_ref[width:], preferred_element_type=jnp.float32)
    for j in range(points // repeat):
        here = slice(j * repeat, (j + 1) * repeat)
        query = q_ref[here].astype(jnp.float32)
        repeated = jnp.concatenate([query] * frames, axis=0)
        square = jnp.sum(repeated * repeated, axis=1, keepdims=True)
        matched = jnp.concatenate([m_ref[f, here] for f in range(frames)], axis=0)
        matched = matched.astype(jnp.float32)
        power = (jnp.sum(matched * matched, axis=1, keepdims=True) + square) * (0.5 / width)
        scale = lax.rsqrt(power + 1e-06)
        wide = jnp.broadcast_to(scale, (side, 128))
        high = wide.astype(jnp.bfloat16)
        normed = jnp.concatenate([(matched * scale).astype(jnp.bfloat16), high], axis=1)
        blend = jnp.dot(mixes_ref[0], normed, preferred_element_type=jnp.float32)
        for part in range(1, mixes_ref.shape[0]):
            blend = blend + jnp.dot(mixes_ref[part], normed, preferred_element_type=jnp.float32)
        section = (matched + blend[:, :width]).astype(jnp.bfloat16).astype(jnp.float32)
        times = 1.0 + blend[:, width:]
        power = (
            jnp.sum(section * section, axis=1, keepdims=True) + times * times * square
        ) * (0.5 / width)
        scale = lax.rsqrt(power + 1e-06)
        inner = (section * jnp.concatenate([scale] * (width // 128), axis=1)).astype(jnp.bfloat16)
        lifted = jnp.concatenate([scale * times] * (step // 128), axis=1)
        lifted = lifted.reshape(frames, repeat, step)
        acc = None
        for h in range(0, hidden, step):
            upper = jnp.dot(
                inner, up_ref[:width, h : h + step], preferred_element_type=jnp.float32
            )
            upper = upper.reshape(frames, repeat, step) + lifted * lift_ref[here, h : h + step][None]
            upper = jax.nn.gelu(upper.reshape(side, step)).astype(jnp.bfloat16)
            part = jnp.dot(upper, down_ref[h : h + step], preferred_element_type=jnp.float32)
            acc = part if acc is None else acc + part
        kept = jnp.concatenate(
            [section, repeated * jnp.concatenate([times] * (width // 128), axis=1)], axis=1
        )
        mixed = (kept + acc).astype(jnp.bfloat16)
        delta = jnp.dot(mixed, tq_ref[...], preferred_element_type=jnp.float32)
        delta = delta.astype(jnp.bfloat16).astype(jnp.float32)
        for f in range(frames):
            out_ref[f, here] = (query + delta[f * repeat : (f + 1) * repeat]).astype(jnp.bfloat16)


def mixer(matched, query, mixes, w_up, w_down, w_query, step=1024):
    tokens = matched.shape[0] * matched.shape[1]
    return pl.pallas_call(
        functools.partial(mixer_kernel, step),
        out_shape=jax.ShapeDtypeStruct(matched.shape, jnp.bfloat16),
        in_specs=[IN_VMEM] * 6,
        out_specs=IN_VMEM,
        scratch_shapes=[pltpu.VMEM((query.shape[0], w_up.shape[1]), jnp.float32)],
        compiler_params=params(18),
        cost_estimate=cost(tokens * (w_up.size + w_down.size), 2 * (w_up.size + w_down.size)),
        name="mixer",
    )(matched, query, mixes, w_up, w_down, w_query)


def ring_pairs(chips, step):
    return [
        (chip * 2 + core, (chip + step) % chips * 2 + core)
        for chip in range(chips)
        for core in range(2)
    ]


def swap_pairs(chips):
    return [(chip * 2 + core, chip * 2 + 1 - core) for chip in range(chips) for core in range(2)]


def shards(feats, query_frame, query_pos, time_mix, w_up, w_down, w_query):
    points = query_frame.shape[0]
    groups = lax.axis_size("tm")
    share = points // groups
    chips = lax.axis_size("pts") // 2
    width = feats.shape[2]
    tile, want = begin(feats[0], query_frame.reshape(1, points), query_pos.reshape(1, points))
    mixes, token = spread_mix(time_mix)
    swap = swap_pairs(chips)
    up, down = ring_pairs(chips, 1), ring_pairs(chips, -1)
    half = chips // 2
    tiles = []
    marks = []
    own = []
    done = 0

    def hold(piece, away, other):
        tiles.append(piece)
        marks.append((away, other))

    def swapped(piece):
        return lax.ppermute(piece, "pts", swap)

    hold(tile, 0, False)
    hold(swapped(tile), 0, True)
    below, above = lax.ppermute(feats[0], "pts", up), lax.ppermute(feats[0], "pts", down)
    for step in range(1, half):
        arrived = [(above, step), (below, -step)]
        below = lax.ppermute(below, "pts", up)
        if step + 1 < half:
            above = lax.ppermute(above, "pts", down)
        for piece, away in arrived:
            hold(piece, away, False)
        sent = [piece for piece, _ in arrived]
        if step == half - 1:
            picked, *sent = pick(want, marks, tiles, own, sent, (token,))
            own = [picked]
            done = len(tiles)
        for piece, (_, away) in zip(sent, arrived):
            hold(swapped(piece), away, True)
    hold(below, -half, False)
    last = swapped(below)
    own = pick(want, marks[done:], tiles[done:], own)
    hold(last, -half, True)
    own = pick(want, marks[-1:], tiles[-1:], own)
    parts = lax.all_to_all(own[0].reshape(groups, share, width), "tm", 0, 0, tiled=True)
    query_here, copies = join(parts)
    query = lax.all_to_all(copies, "tm", 0, 0, tiled=True).reshape(points, width)
    matched = match(query, tiles).reshape(groups, share, width)
    matched = lax.all_to_all(matched, "tm", 0, 0, tiled=True)
    refined = mixer(matched, query_here, mixes, w_up, w_down, w_query)
    refined = lax.all_to_all(refined, "tm", 0, 0, tiled=True).reshape(points, width)
    return rematch(refined, marks, tiles)


def solution(mesh):
    placed = (P("tm", "pts", None), P("pts"), P("pts"), P(), P(), P(), P())
    return jax.shard_map(
        shards,
        mesh=mesh,
        in_specs=placed,
        out_specs=(P("tm", "pts"), P("tm", "pts")),
        check_vma=False,
    )
```
